32 devices in a mesh: group: 4 (over y, core), dp: 8 (over z, x).
Axes of the slice: x: 2, y: 2, z: 4, core: 2. Of those that a mesh axis runs over, the one named last changes fastest.
Arguments:
- table: bfloat16 [16384, 1024], P(('group', 'dp')), may hold values from -6 to 6
- accum: float32 [16384], P(('group', 'dp')), may hold values from 0.05 to 5
- pair_block: int32 [1024], P(('group', 'dp')), may hold values from 0 to 127, as said below
- pair_protein: int32 [1024], P(('group', 'dp')), may hold values from 0 to 127, as said below
- pair_weight: bfloat16 [1024, 128], P(('group', 'dp')), may hold values from 0 to 1, as said below
- w_hidden: bfloat16 [1024, 1024], replicated, may hold values from -0.1875 to 0.1875
- hidden_cot: bfloat16 [128, 1024], P(('group', 'dp')), may hold values from -6 to 6
Outputs:
- new_table: bfloat16 [16384, 1024], P(('group', 'dp'))
- new_accum: float32 [16384], P(('group', 'dp'))
The draws below stay inside these ranges and needn't reach their ends.
Inputs may be any that keep to these rules, and one draw needn't show every extreme that they name: `pair_block`: the owner of block b is device b // 4 along group+dp. Of one device's 32 pairs at most 2 name blocks of one owner; every device reaches 2 for some owner, and some owner receives 2 pairs from every device. `pair_protein`: A device's pairs name only that device's proteins (index // 4 is the device's index along group+dp), each of them at least once. `pair_weight`: Nonnegative; every pair has at least one positive weight.
All inputs are finite; a program needn't handle non-finite values.
Results may differ from the reference program's by a relative error of at most 0.001.
Values may be sent and summed in bfloat16 or wider, within the bound.
A program may use at most 64 MiB of HBM per device.

```python
import math
import jax
import jax.numpy as jnp
from jax import lax

D = 1024
H = 1024
BLOCK = 128
BLK_DEV = 4
CAP = 2
P_DEV = 4
ROWS_DEV = 512
ROWS = 16384
PAIRS_DEV = 32
PAIRS = 1024
PROTEINS = 128
N_GROUP = 4
N_DP = 8


def draw_pair_block(key, part):
    key = jax.random.fold_in(key, 11)
    count = N_GROUP * N_DP
    chosen = PAIRS_DEV // CAP
    key_hot, key_perm, key_local = jax.random.split(key, 3)
    hot_rank = jax.random.permutation(key_hot, count)
    hot_flag = (hot_rank < max(1, count // 16)).astype(jnp.int32)
    perms = jax.vmap(lambda k: jax.random.permutation(k, count))(jax.random.split(key_perm, count))
    scores = hot_flag[None, :] * count + perms.astype(jnp.int32)
    top_scores, owners = lax.top_k(scores, chosen)
    owners = jnp.repeat(owners.astype(jnp.int32), CAP, axis=1)
    local = jax.random.randint(key_local, (count, PAIRS_DEV), 0, BLK_DEV)
    return (owners * BLK_DEV + local).reshape(-1).astype(jnp.int32)


def draw_pair_protein(key, part):
    key = jax.random.fold_in(key, 12)
    count = N_GROUP * N_DP
    key_one, key_two = jax.random.split(key)
    first = jax.random.randint(key_one, (count, PAIRS_DEV), 0, P_DEV)
    second = jax.random.randint(key_two, (count, PAIRS_DEV), 0, P_DEV)
    local = jnp.minimum(first, second)
    local = local.at[:, :P_DEV].set(jnp.arange(P_DEV, dtype=jnp.int32)[None, :])
    offsets = jnp.arange(count, dtype=jnp.int32)[:, None] * P_DEV
    return (local + offsets).reshape(-1).astype(jnp.int32)


def draw_pair_weight(key, part):
    key = jax.random.fold_in(key, 13)
    key_keep, key_vals, key_first = jax.random.split(key, 3)
    sure_row = jax.random.randint(key_first, (PAIRS, 1), 0, BLOCK)
    columns = jnp.arange(BLOCK, dtype=jnp.int32)[None, :]
    keep = jax.random.bernoulli(key_keep, 0.02, (PAIRS, BLOCK)) | (columns == sure_row)
    values = jnp.exp(jax.random.uniform(key_vals, (PAIRS, BLOCK), jnp.float32, jnp.log(0.05), 0.0))
    return jnp.where(keep, values, 0.0).astype(jnp.float32).astype(jnp.bfloat16)


def level_of(rng, shape, pieces, low, largest):
    factor_of = 1.0
    for dim, shards_of in pieces:
        steps = jax.random.uniform(jax.random.fold_in(jax.random.fold_in(rng, 6), dim), (shards_of,), jnp.float32, low / len(pieces), largest / len(pieces))
        factor_of = factor_of * jnp.repeat(jnp.exp(steps), shape[dim] // shards_of).reshape((-1,) + (1,) * (len(shape) - 1 - dim))
    return factor_of


def noise(key, shape, scale, limit, shards=(), kind=jnp.bfloat16):
    level = level_of(key, shape, shards, -0.22, 0.18) if shards else 1.0
    result = jax.random.normal(key, shape, jnp.float32) * scale * level
    return jnp.minimum(jnp.maximum(result, -limit), limit).astype(kind)


def setup_inputs(seed: int = 0) -> dict:
    key_list = jax.random.split(jax.random.key(seed), 8)
    table = noise(key_list[0], (ROWS, D), 1.0, 6.0, ((0, 32),))
    accum = jnp.clip(jnp.exp(math.log(5.0) - 4.6051702 * jax.random.uniform(key_list[1], (ROWS,), jnp.float32) ** level_of(key_list[1], (ROWS,), ((0, 32),), -0.2, 0.2)), 0.05, 5.0)
    pair_block = draw_pair_block(jax.random.fold_in(key_list[7], 71), 0)
    pair_protein = draw_pair_protein(jax.random.fold_in(key_list[7], 71), 0)
    pair_weight = draw_pair_weight(jax.random.fold_in(key_list[7], 71), 0)
    w_hidden = noise(key_list[5], (D, H), D ** -0.5, 0.1875)
    hidden_cot = noise(key_list[6], (PROTEINS, H), 1.0, 6.0, ((0, 32),))
    return {"table": table, "accum": accum, "pair_block": pair_block, "pair_protein": pair_protein, "pair_weight": pair_weight, "w_hidden": w_hidden, "hidden_cot": hidden_cot}


def mlp_grad(bag, w_hidden, hidden_cot):
    inv = lax.rsqrt(lax.optimization_barrier(jnp.mean(bag * bag, axis=-1, keepdims=True)) + 1e-06)
    unit = bag * inv
    unit_b = unit.astype(jnp.bfloat16)
    pre = jnp.dot(unit_b, w_hidden, preferred_element_type=jnp.float32)
    sig = jax.nn.sigmoid(pre)
    dpre = (hidden_cot.astype(jnp.float32) * sig * (1.0 + pre * (1.0 - sig))).astype(jnp.bfloat16)
    dunit = lax.dot_general(dpre, w_hidden, (((1,), (1,)), ((), ())), preferred_element_type=jnp.float32)
    dbag = (dunit - unit * lax.optimization_barrier(jnp.mean(dunit * unit, axis=-1, keepdims=True))) * inv
    return dbag.astype(jnp.bfloat16)

def expand_dense(weights, blocks, count):
    hit = blocks[:, None, None] == jnp.arange(count, dtype=jnp.int32)[None, :, None]
    dense = jnp.where(hit, weights[:, None, :], jnp.zeros((), weights.dtype))
    return dense.reshape(weights.shape[0], count * weights.shape[1])

def reference(table, accum, pair_block, pair_protein, pair_weight, w_hidden, hidden_cot):
    devices = N_GROUP * N_DP
    slots = CAP * devices
    owner = (pair_block // BLK_DEV).astype(jnp.int32)
    order = jnp.argsort(owner, stable=True)
    s_owner = owner[order]
    s_blk = jnp.concatenate([(pair_block % BLK_DEV).astype(jnp.int32)[order], jnp.zeros((slots,), jnp.int32)])
    s_pid = jnp.concatenate([pair_protein.astype(jnp.int32)[order], jnp.zeros((slots,), jnp.int32)])
    s_w = jnp.concatenate([pair_weight[order], jnp.zeros((slots, BLOCK), pair_weight.dtype)])
    targets = jnp.arange(devices, dtype=jnp.int32)
    starts = jnp.searchsorted(s_owner, targets, side='left').astype(jnp.int32)
    ends = jnp.searchsorted(s_owner, targets, side='right').astype(jnp.int32)
    tables = table.reshape(devices, ROWS_DEV, D)
    accums = accum.reshape(devices, ROWS_DEV)

    def window(owner_id):
        begin = starts[owner_id]
        valid = begin + jnp.arange(slots, dtype=jnp.int32) < ends[owner_id]
        weights = lax.dynamic_slice(s_w, (begin, jnp.int32(0)), (slots, BLOCK))
        weights = jnp.where(valid[:, None], weights, jnp.zeros((), weights.dtype))
        blocks = lax.dynamic_slice(s_blk, (begin,), (slots,))
        pids = lax.dynamic_slice(s_pid, (begin,), (slots,))
        return (expand_dense(weights, blocks, BLK_DEV), pids, valid)

    def forward(bag, inputs):
        owner_id, rows = inputs
        dense, pids, valid = window(owner_id)
        partial_value = jnp.dot(dense, rows, preferred_element_type=jnp.float32).astype(jnp.bfloat16).astype(jnp.float32)
        partial_value = jnp.where(valid[:, None], partial_value, jnp.zeros((), jnp.float32))
        return (bag.at[pids].add(partial_value), None)
    bag, _ = lax.scan(forward, jnp.zeros((PROTEINS, D), jnp.float32), (targets, tables))
    dbag = mlp_grad(bag, w_hidden, hidden_cot)

    def backward(inputs):
        owner_id, rows, acc = inputs
        dense, pids, valid = window(owner_id)
        grads = dbag[pids]
        grad = lax.dot_general(dense, grads, (((0,), (0,)), ((), ())), preferred_element_type=jnp.float32)
        acc_new = acc + lax.optimization_barrier(jnp.mean(grad * grad, axis=-1))
        rows_new = rows.astype(jnp.float32) - 0.3 * grad / (jnp.sqrt(acc_new)[:, None] + 1e-08)
        return (rows_new.astype(jnp.bfloat16), acc_new)
    new_rows, new_acc = lax.map(backward, (targets, tables, accums))
    return (new_rows.reshape(ROWS, D), new_acc.reshape(ROWS))
```

```python
import functools

import jax
import jax.numpy as jnp
from jax import lax
from jax.experimental import pallas as pl
from jax.experimental.pallas import tpu as pltpu
from jax.sharding import PartitionSpec as P

CAP = 2
LANES = 128
TOGETHER = 16
PAD = 8
MESH = pl.DeviceIdType.MESH
BF = jnp.bfloat16
F32 = jnp.float32


def dot(a, b):
    return jnp.dot(a, b, preferred_element_type=F32)


def dot_nt(a, b):
    return lax.dot_general(a, b, (((1,), (1,)), ((), ())), preferred_element_type=F32)


def iota(shape, dim):
    return lax.broadcasted_iota(jnp.int32, shape, dim)


def ones_where(mask):
    return jnp.where(mask, 1.0, 0.0).astype(BF)


def kernel(
    n_group,
    n_dp,
    blk_ref,
    prot_ref,
    w_ref,
    cot_ref,
    accum_ref,
    table_hbm,
    hid_hbm,
    out_hbm,
    acc_ref,
    table,
    hid,
    rows_out,
    send_w,
    got_w,
    send_part,
    got_part,
    send_grad,
    got_grad,
    dense,
    dense_t,
    gathered,
    pick,
    pick_t,
    sends,
    recvs,
    loads,
    stores,
):
    n = n_group * n_dp
    me = lax.axis_index("group") * n_dp + lax.axis_index("dp")
    load_table = pltpu.make_async_copy(table_hbm, table, loads.at[0])
    load_hid = pltpu.make_async_copy(hid_hbm, hid, loads.at[1])
    load_table.start()
    load_hid.start()

    def where_is(t):
        return (lax.div(t, n_dp), lax.rem(t, n_dp))

    barrier = pltpu.get_barrier_semaphore()

    def greet(i, carry):
        t = lax.rem(me + i, n)
        pl.semaphore_signal(barrier, inc=1, device_id=where_is(t), device_id_type=MESH)
        return carry

    lax.fori_loop(1, n, greet, 0)

    def exchange(send, got, phase):
        def start(i, carry):
            t = lax.rem(me + i, n)
            pltpu.make_async_remote_copy(
                src_ref=send.at[t],
                dst_ref=got.at[me],
                send_sem=sends.at[phase],
                recv_sem=recvs.at[phase],
                device_id=where_is(t),
                device_id_type=MESH,
            ).start()
            return carry

        lax.fori_loop(1, n, start, 0)
        got[me] = send[me]

    others = pl.ds(0, n - 1)

    def arrived(got, phase):
        pltpu.make_async_copy(got.at[others], got.at[others], recvs.at[phase]).wait()

    def left(send, phase):
        pltpu.make_async_copy(send.at[others], send.at[others], sends.at[phase]).wait()

    width = table.shape[1]
    block_rows = w_ref.shape[1]
    blocks = table.shape[0] // block_rows
    chunks = width // LANES
    proteins = cot_ref.shape[0]
    pairs = w_ref.shape[0]
    tile = chunks * CAP
    slots = n * CAP
    step = min(TOGETHER, n)
    groups = n // step
    rows = step * tile
    few = groups <= 4

    def each(body):
        if few:
            for g in range(groups):
                body(g)
        else:
            lax.fori_loop(0, groups, lambda g, c: (body(g), c)[1], 0)

    def at(g, size):
        return pl.ds(g * size, size) if few else pl.ds(pl.multiple_of(g * size, size), size)

    blk = blk_ref[...]
    owner = lax.div(blk, blocks)
    local = lax.rem(blk, blocks)
    local_prot = prot_ref[...] - me * proteins
    square = (pairs, pairs)
    from_row, from_col = iota(square, 0), iota(square, 1)
    owner_f = owner.astype(F32)
    owner_col = jnp.sum(jnp.where(from_row == from_col, owner_f, 0.0), axis=1, keepdims=True)
    earlier = (owner_col == owner_f) & (from_row < from_col)
    rank = jnp.sum(jnp.where(earlier, 1.0, 0.0), axis=0, keepdims=True)
    slot = owner * CAP + rank.astype(jnp.int32)

    place_rows = iota((rows, pairs), 0)
    place_c = lax.rem(place_rows, tile) // CAP
    place_slot = (place_rows // tile) * CAP + lax.rem(place_rows, CAP)
    for_prot = ones_where(iota((chunks * PAD, pairs), 0) % PAD == local_prot)
    same_c = iota((chunks * PAD, rows), 0) // PAD == (iota((chunks * PAD, rows), 1) % tile) // CAP
    same_c_t = iota((rows, chunks * PAD), 1) // PAD == (iota((rows, chunks * PAD), 0) % tile) // CAP
    weights = w_ref[...]

    def place_of(g):
        return place_slot + g * (step * CAP) == slot

    def make_w(g):
        place = place_of(g) & (place_c == local)
        send_w[at(g, step)] = dot(ones_where(place), weights).astype(BF).reshape(step, tile, LANES)

    each(make_w)
    pl.semaphore_wait(barrier, n - 1)
    exchange(send_w, got_w, 0)

    def make_pick(g):
        place = ones_where(place_of(g))
        pick[g] = jnp.where(same_c, dot_nt(for_prot, place), 0.0).astype(BF)
        pick_t[at(g, rows), :] = jnp.where(same_c_t, dot_nt(place, for_prot), 0.0).astype(BF)

    each(make_pick)

    to_r, to_c = iota((rows, rows), 0), iota((rows, rows), 1)
    stacked = step * CAP
    r_c, r_d, r_k = to_r // stacked, (to_r % stacked) // CAP, to_r % CAP
    unpack = ones_where(to_c == r_d * tile + r_c * CAP + r_k)
    t_c, t_d, t_k = to_c // stacked, (to_c % stacked) // CAP, to_c % CAP
    pack = ones_where(to_r == t_d * tile + t_c * CAP + t_k)

    def unpacked(got, g, count):
        flat = got[at(g, step)].reshape(rows, LANES)
        high = dot(unpack[: count * stacked], flat)
        return jnp.concatenate(
            [high[c * stacked : (c + 1) * stacked] for c in range(count)], axis=1
        )

    arrived(got_w, 0)

    def make_dense(g):
        dense[at(g, stacked), :] = unpacked(got_w, g, blocks * block_rows // LANES).astype(BF)

    each(make_dense)
    load_table.wait()
    big = min(slots, 256)
    per_big = big // stacked

    def make_part(h):
        some = dense[pl.ds(h * big if few else pl.multiple_of(h * big, big), big), :]
        part = dot(some, table[...]).astype(BF)
        for j in range(per_big):
            own = part[j * stacked : (j + 1) * stacked]
            stack = jnp.concatenate(
                [own[:, c * LANES : (c + 1) * LANES] for c in range(chunks)], axis=0
            )
            send_part[at(h * per_big + j, step)] = (
                dot(pack, stack).astype(BF).reshape(step, tile, LANES)
            )

    if few:
        for h in range(slots // big):
            make_part(h)
    else:
        lax.fori_loop(0, slots // big, lambda h, c: (make_part(h), c)[1], 0)
    exchange(send_part, got_part, 1)

    dense_t[...] = dense[...].astype(F32).T.astype(BF)
    load_hid.wait()
    arrived(got_part, 1)

    def bag_of(g):
        return dot(pick[g], got_part[at(g, step)].reshape(rows, LANES))

    if few:
        stack = sum(bag_of(g) for g in range(groups))
    else:
        stack = lax.fori_loop(
            0, groups, lambda g, c: c + bag_of(g), jnp.zeros((chunks * PAD, LANES), F32)
        )
    bag = jnp.concatenate([stack[c * PAD : (c + 1) * PAD] for c in range(chunks)], axis=1)
    cot = cot_ref[...].astype(F32)
    cot = jnp.concatenate([cot, jnp.zeros((PAD - proteins, cot.shape[1]), F32)], axis=0)
    inv = lax.rsqrt(jnp.mean(bag * bag, axis=-1, keepdims=True) + 1e-06)
    unit = bag * inv
    pre = dot(unit.astype(BF), hid[...])
    sig = jax.nn.sigmoid(pre)
    dpre = (cot * sig * (1.0 + pre * (1.0 - sig))).astype(BF)
    dunit = dot_nt(dpre, hid[...])
    dbag = (dunit - unit * jnp.mean(dunit * unit, axis=-1, keepdims=True)) * inv
    dstack = jnp.concatenate(
        [dbag[:, c * LANES : (c + 1) * LANES] for c in range(chunks)], axis=0
    ).astype(BF)

    def make_grad(g):
        send_grad[at(g, step)] = (
            dot(pick_t[at(g, rows), :], dstack).astype(BF).reshape(step, tile, LANES)
        )

    each(make_grad)
    exchange(send_grad, got_grad, 2)
    left(send_w, 0)
    left(send_part, 1)
    arrived(got_grad, 2)

    def make_gathered(g):
        gathered[at(g, stacked), :] = unpacked(got_grad, g, chunks).astype(BF)

    each(make_gathered)
    diagonal = iota((block_rows, block_rows), 0) == iota((block_rows, block_rows), 1)
    writes = []
    for b in range(blocks):
        some = pl.ds(b * block_rows, block_rows)
        grad = dot(dense_t[some, :], gathered[...])
        mean = jnp.mean(grad * grad, axis=-1, keepdims=True)
        old = jnp.sum(jnp.where(diagonal, accum_ref[b : b + 1, :], 0.0), axis=1, keepdims=True)
        new = old + mean
        scale = 0.3 / (jnp.sqrt(new) + 1e-08)
        rows_out[some, :] = (table[some, :].astype(F32) - grad * scale).astype(BF)
        write = pltpu.make_async_copy(rows_out.at[some], out_hbm.at[some], stores.at[b])
        write.start()
        writes.append(write)
        acc_ref[b : b + 1, :] = jnp.sum(jnp.where(diagonal, new, 0.0), axis=0, keepdims=True)
    left(send_grad, 2)
    for write in writes:
        write.wait()


def per_device(table, accum, pair_block, pair_protein, pair_weight, w_hidden, hidden_cot):
    n_group = lax.axis_size("group")
    n_dp = lax.axis_size("dp")
    n = n_group * n_dp
    rows_dev, width = table.shape
    pairs, block_rows = pair_weight.shape
    blocks = rows_dev // block_rows
    tile = (width // LANES) * CAP
    slots = n * CAP
    step = min(TOGETHER, n)
    vmem = pl.BlockSpec(memory_space=pltpu.VMEM)
    hbm = pl.BlockSpec(memory_space=pl.ANY)
    tiles = pltpu.VMEM((n, tile, LANES), BF)
    stack = (width // LANES) * PAD
    new_table, new_accum = pl.pallas_call(
        functools.partial(kernel, n_group, n_dp),
        out_shape=(
            jax.ShapeDtypeStruct(table.shape, BF),
            jax.ShapeDtypeStruct((blocks, block_rows), F32),
        ),
        in_specs=[vmem] * 5 + [hbm] * 2,
        out_specs=(hbm, vmem),
        scratch_shapes=[
            pltpu.VMEM(table.shape, BF),
            pltpu.VMEM(w_hidden.shape, BF),
            pltpu.VMEM(table.shape, BF),
            tiles,
            tiles,
            tiles,
            tiles,
            tiles,
            tiles,
            pltpu.VMEM((slots, rows_dev), BF),
            pltpu.VMEM((rows_dev, slots), BF),
            pltpu.VMEM((slots, width), BF),
            pltpu.VMEM((n // step, stack, step * tile), BF),
            pltpu.VMEM((n * tile, stack), BF),
            pltpu.SemaphoreType.DMA((3,)),
            pltpu.SemaphoreType.DMA((3,)),
            pltpu.SemaphoreType.DMA((2,)),
            pltpu.SemaphoreType.DMA((blocks,)),
        ],
        compiler_params=pltpu.CompilerParams(
            collective_id=0, has_side_effects=True, vmem_limit_bytes=48 * 1024 * 1024
        ),
        name="bags",
    )(
        pair_block.reshape(1, pairs),
        pair_protein.reshape(1, pairs),
        pair_weight,
        hidden_cot,
        accum.reshape(blocks, block_rows),
        table,
        w_hidden,
    )
    return new_table, new_accum.reshape(rows_dev)


def solution(mesh):
    in_specs = (
        P(("group", "dp"), None),
        P(("group", "dp")),
        P(("group", "dp")),
        P(("group", "dp")),
        P(("group", "dp"), None),
        P(),
        P(("group", "dp"), None),
    )
    out_specs = (P(("group", "dp"), None), P(("group", "dp")))
    return jax.shard_map(
        per_device, mesh=mesh, in_specs=in_specs, out_specs=out_specs, check_vma=False
    )
```

```python
import functools

import jax
import jax.numpy as jnp
from jax import lax
from jax.experimental import pallas as pl
from jax.experimental.pallas import tpu as pltpu
from jax.sharding import PartitionSpec as P

CAP = 2
LANES = 128
TOGETHER = 16
PAD = 8
LIMIT = 64 * 1024 * 1024
MESH = pl.DeviceIdType.MESH
BF = jnp.bfloat16
F32 = jnp.float32


def dot(a, b):
    return jnp.dot(a, b, preferred_element_type=F32)


def dot_nt(a, b):
    return lax.dot_general(a, b, (((1,), (1,)), ((), ())), preferred_element_type=F32)


def iota(shape, dim):
    return lax.broadcasted_iota(jnp.int32, shape, dim)


def ones_where(mask):
    return jnp.where(mask, 1.0, 0.0).astype(BF)


def kernel(
    n_group,
    n_dp,
    blk_hbm,
    prot_hbm,
    w_hbm,
    cot_hbm,
    accum_hbm,
    table_hbm,
    hid_hbm,
    out_hbm,
    acc_hbm,
    blk_ref,
    prot_ref,
    w_ref,
    cot_ref,
    accum_ref,
    table,
    hid,
    acc_ref,
    rows_out,
    send_w,
    got_w,
    send_part,
    got_part,
    send_grad,
    got_grad,
    dense,
    dense_t,
    gathered,
    pick,
    pick_t,
    sends,
    recvs,
    loads,
    stores,
):
    n = n_group * n_dp
    me = lax.axis_index("group") * n_dp + lax.axis_index("dp")
    pairs_of = [(blk_hbm, blk_ref), (prot_hbm, prot_ref), (w_hbm, w_ref)]
    others_of = [(table_hbm, table), (hid_hbm, hid), (cot_hbm, cot_ref), (accum_hbm, accum_ref)]
    copies = [
        pltpu.make_async_copy(a, b, loads.at[i]) for i, (a, b) in enumerate(pairs_of + others_of)
    ]
    for copy in copies:
        copy.start()
    load_pairs = copies[:3]
    load_table, load_hid, load_cot, load_accum = copies[3:]

    def where_is(t):
        return (lax.div(t, n_dp), lax.rem(t, n_dp))

    barrier = pltpu.get_barrier_semaphore()

    def greet(i, carry):
        t = lax.rem(me + i, n)
        pl.semaphore_signal(barrier, inc=1, device_id=where_is(t), device_id_type=MESH)
        return carry

    lax.fori_loop(1, n, greet, 0)

    def exchange(send, got, phase):
        def start(i, carry):
            t = lax.rem(me + i, n)
            pltpu.make_async_remote_copy(
                src_ref=send.at[t],
                dst_ref=got.at[me],
                send_sem=sends.at[phase],
                recv_sem=recvs.at[phase],
                device_id=where_is(t),
                device_id_type=MESH,
            ).start()
            return carry

        lax.fori_loop(1, n, start, 0)
        got[me] = send[me]

    others = pl.ds(0, n - 1)

    def arrived(got, phase):
        pltpu.make_async_copy(got.at[others], got.at[others], recvs.at[phase]).wait()

    def left(send, phase):
        pltpu.make_async_copy(send.at[others], send.at[others], sends.at[phase]).wait()

    width = table.shape[1]
    block_rows = w_ref.shape[1]
    blocks = table.shape[0] // block_rows
    chunks = width // LANES
    proteins = cot_ref.shape[0]
    pairs = w_ref.shape[0]
    tile = chunks * CAP
    slots = n * CAP
    step = min(TOGETHER, n)
    groups = n // step
    rows = step * tile
    few = groups <= 4

    def each(body):
        if few:
            for g in range(groups):
                body(g)
        else:
            lax.fori_loop(0, groups, lambda g, c: (body(g), c)[1], 0)

    def at(g, size):
        return pl.ds(g * size, size) if few else pl.ds(pl.multiple_of(g * size, size), size)

    for copy in load_pairs:
        copy.wait()
    blk = blk_ref[...]
    owner = lax.div(blk, blocks)
    local = lax.rem(blk, blocks)
    local_prot = prot_ref[...] - me * proteins
    square = (pairs, pairs)
    from_row, from_col = iota(square, 0), iota(square, 1)
    owner_f = owner.astype(F32)
    owner_col = jnp.sum(jnp.where(from_row == from_col, owner_f, 0.0), axis=1, keepdims=True)
    earlier = (owner_col == owner_f) & (from_row < from_col)
    rank = jnp.sum(jnp.where(earlier, 1.0, 0.0), axis=0, keepdims=True)
    slot = owner * CAP + rank.astype(jnp.int32)

    place_rows = iota((rows, pairs), 0)
    place_c = lax.rem(place_rows, tile) // CAP
    place_slot = (place_rows // tile) * CAP + lax.rem(place_rows, CAP)
    for_prot = ones_where(iota((chunks * PAD, pairs), 0) % PAD == local_prot)
    same_c = iota((chunks * PAD, rows), 0) // PAD == (iota((chunks * PAD, rows), 1) % tile) // CAP
    same_c_t = iota((rows, chunks * PAD), 1) // PAD == (iota((rows, chunks * PAD), 0) % tile) // CAP
    weights = w_ref[...]

    def place_of(g):
        return place_slot + g * (step * CAP) == slot

    def make_w(g):
        place = place_of(g) & (place_c == local)
        send_w[at(g, step)] = dot(ones_where(place), weights).astype(BF).reshape(step, tile, LANES)

    each(make_w)
    pl.semaphore_wait(barrier, n - 1)
    exchange(send_w, got_w, 0)

    def make_pick(g):
        place = ones_where(place_of(g))
        pick[g] = jnp.where(same_c, dot_nt(for_prot, place), 0.0).astype(BF)
        pick_t[at(g, rows), :] = jnp.where(same_c_t, dot_nt(place, for_prot), 0.0).astype(BF)

    each(make_pick)

    to_r, to_c = iota((rows, rows), 0), iota((rows, rows), 1)
    stacked = step * CAP
    r_c, r_d, r_k = to_r // stacked, (to_r % stacked) // CAP, to_r % CAP
    unpack = ones_where(to_c == r_d * tile + r_c * CAP + r_k)
    t_c, t_d, t_k = to_c // stacked, (to_c % stacked) // CAP, to_c % CAP
    pack = ones_where(to_r == t_d * tile + t_c * CAP + t_k)

    def unpacked(got, g, count):
        flat = got[at(g, step)].reshape(rows, LANES)
        high = dot(unpack[: count * stacked], flat)
        return jnp.concatenate(
            [high[c * stacked : (c + 1) * stacked] for c in range(count)], axis=1
        )

    arrived(got_w, 0)

    def make_dense(g):
        dense[at(g, stacked), :] = unpacked(got_w, g, blocks * block_rows // LANES).astype(BF)

    each(make_dense)
    load_table.wait()
    big = min(slots, 256)
    per_big = big // stacked

    def make_part(h):
        some = dense[pl.ds(h * big if few else pl.multiple_of(h * big, big), big), :]
        part = dot(some, table[...]).astype(BF)
        for j in range(per_big):
            own = part[j * stacked : (j + 1) * stacked]
            stack = jnp.concatenate(
                [own[:, c * LANES : (c + 1) * LANES] for c in range(chunks)], axis=0
            )
            send_part[at(h * per_big + j, step)] = (
                dot(pack, stack).astype(BF).reshape(step, tile, LANES)
            )

    if few:
        for h in range(slots // big):
            make_part(h)
    else:
        lax.fori_loop(0, slots // big, lambda h, c: (make_part(h), c)[1], 0)
    exchange(send_part, got_part, 1)

    dense_t[...] = dense[...].astype(F32).T.astype(BF)
    load_hid.wait()
    load_accum.wait()
    arrived(got_part, 1)

    def bag_of(g):
        return dot(pick[g], got_part[at(g, step)].reshape(rows, LANES))

    if few:
        stack = sum(bag_of(g) for g in range(groups))
    else:
        stack = lax.fori_loop(
            0, groups, lambda g, c: c + bag_of(g), jnp.zeros((chunks * PAD, LANES), F32)
        )
    bag = jnp.concatenate([stack[c * PAD : (c + 1) * PAD] for c in range(chunks)], axis=1)
    load_cot.wait()
    cot = cot_ref[...].astype(F32)
    cot = jnp.concatenate([cot, jnp.zeros((PAD - proteins, cot.shape[1]), F32)], axis=0)
    inv = lax.rsqrt(jnp.mean(bag * bag, axis=-1, keepdims=True) + 1e-06)
    unit = bag * inv
    pre = dot(unit.astype(BF), hid[...])
    sig = jax.nn.sigmoid(pre)
    dpre = (cot * sig * (1.0 + pre * (1.0 - sig))).astype(BF)
    dunit = dot_nt(dpre, hid[...])
    dbag = (dunit - unit * jnp.mean(dunit * unit, axis=-1, keepdims=True)) * inv
    dstack = jnp.concatenate(
        [dbag[:, c * LANES : (c + 1) * LANES] for c in range(chunks)], axis=0
    ).astype(BF)

    def make_grad(g):
        send_grad[at(g, step)] = (
            dot(pick_t[at(g, rows), :], dstack).astype(BF).reshape(step, tile, LANES)
        )

    each(make_grad)
    exchange(send_grad, got_grad, 2)
    left(send_w, 0)
    left(send_part, 1)
    arrived(got_grad, 2)

    def make_gathered(g):
        gathered[at(g, stacked), :] = unpacked(got_grad, g, chunks).astype(BF)

    each(make_gathered)
    diagonal = iota((block_rows, block_rows), 0) == iota((block_rows, block_rows), 1)
    writes = []
    for b in range(blocks):
        some = pl.ds(b * block_rows, block_rows)
        grad = dot(dense_t[some, :], gathered[...])
        mean = jnp.mean(grad * grad, axis=-1, keepdims=True)
        old = jnp.sum(jnp.where(diagonal, accum_ref[b : b + 1, :], 0.0), axis=1, keepdims=True)
        new = old + mean
        scale = 0.3 / (jnp.sqrt(new) + 1e-08)
        rows_out[some, :] = (table[some, :].astype(F32) - grad * scale).astype(BF)
        write = pltpu.make_async_copy(rows_out.at[some], out_hbm.at[some], stores.at[b])
        write.start()
        writes.append(write)
        acc_ref[b : b + 1, :] = jnp.sum(jnp.where(diagonal, new, 0.0), axis=0, keepdims=True)
    write = pltpu.make_async_copy(acc_ref, acc_hbm, stores.at[blocks])
    write.start()
    writes.append(write)
    left(send_grad, 2)
    for write in writes:
        write.wait()


def per_device(table, accum, pair_block, pair_protein, pair_weight, w_hidden, hidden_cot):
    n_group = lax.axis_size("group")
    n_dp = lax.axis_size("dp")
    n = n_group * n_dp
    rows_dev, width = table.shape
    pairs, block_rows = pair_weight.shape
    blocks = rows_dev // block_rows
    tile = (width // LANES) * CAP
    slots = n * CAP
    step = min(TOGETHER, n)
    hbm = pl.BlockSpec(memory_space=pl.ANY)
    tiles = pltpu.VMEM((n, tile, LANES), BF)
    stack = (width // LANES) * PAD
    new_table, new_accum = pl.pallas_call(
        functools.partial(kernel, n_group, n_dp),
        out_shape=(
            jax.ShapeDtypeStruct(table.shape, BF),
            jax.ShapeDtypeStruct((blocks, block_rows), F32),
        ),
        in_specs=[hbm] * 7,
        out_specs=(hbm, hbm),
        scratch_shapes=[
            pltpu.VMEM((1, pairs), jnp.int32),
            pltpu.VMEM((1, pairs), jnp.int32),
            pltpu.VMEM(pair_weight.shape, BF),
            pltpu.VMEM(hidden_cot.shape, BF),
            pltpu.VMEM((blocks, block_rows), F32),
            pltpu.VMEM(table.shape, BF),
            pltpu.VMEM(w_hidden.shape, BF),
            pltpu.VMEM((blocks, block_rows), F32),
            pltpu.VMEM(table.shape, BF),
            tiles,
            tiles,
            tiles,
            tiles,
            tiles,
            tiles,
            pltpu.VMEM((slots, rows_dev), BF),
            pltpu.VMEM((rows_dev, slots), BF),
            pltpu.VMEM((slots, width), BF),
            pltpu.VMEM((n // step, stack, step * tile), BF),
            pltpu.VMEM((n * tile, stack), BF),
            pltpu.SemaphoreType.DMA((3,)),
            pltpu.SemaphoreType.DMA((3,)),
            pltpu.SemaphoreType.DMA((7,)),
            pltpu.SemaphoreType.DMA((blocks + 1,)),
        ],
        compiler_params=pltpu.CompilerParams(
            collective_id=0, has_side_effects=True, vmem_limit_bytes=LIMIT
        ),
        name="bags",
    )(
        pair_block.reshape(1, pairs),
        pair_protein.reshape(1, pairs),
        pair_weight,
        hidden_cot,
        accum.reshape(blocks, block_rows),
        table,
        w_hidden,
    )
    return new_table, new_accum.reshape(rows_dev)


def solution(mesh):
    in_specs = (
        P(("group", "dp"), None),
        P(("group", "dp")),
        P(("group", "dp")),
        P(("group", "dp")),
        P(("group", "dp"), None),
        P(),
        P(("group", "dp"), None),
    )
    out_specs = (P(("group", "dp"), None), P(("group", "dp")))
    return jax.shard_map(
        per_device, mesh=mesh, in_specs=in_specs, out_specs=out_specs, check_vma=False
    )
```

```python
import functools

import jax
import jax.numpy as jnp
from jax import lax
from jax.experimental import pallas as pl
from jax.experimental.pallas import tpu as pltpu
from jax.sharding import PartitionSpec as P

CAP = 2
LANES = 128
TOGETHER = 16
PAD = 8
LIMIT = 64 * 1024 * 1024
MESH = pl.DeviceIdType.MESH
BF = jnp.bfloat16
F32 = jnp.float32


def dot(a, b):
    return jnp.dot(a, b, preferred_element_type=F32)


def dot_nt(a, b):
    return lax.dot_general(a, b, (((1,), (1,)), ((), ())), preferred_element_type=F32)


def iota(shape, dim):
    return lax.broadcasted_iota(jnp.int32, shape, dim)


def ones_where(mask):
    return jnp.where(mask, 1.0, 0.0).astype(BF)


def repack(step, chunks):
    tile, stacked = chunks * CAP, step * CAP
    shape = (step * tile, step * tile)
    to_r, to_c = iota(shape, 0), iota(shape, 1)
    r_c, r_d, r_k = to_r // stacked, (to_r % stacked) // CAP, to_r % CAP
    unpack = ones_where(to_c == r_d * tile + r_c * CAP + r_k)
    t_c, t_d, t_k = to_c // stacked, (to_c % stacked) // CAP, to_c % CAP
    pack = ones_where(to_r == t_d * tile + t_c * CAP + t_k)
    return pack, unpack


def unpacked(unpack, tiles, count):
    step, tile, lanes = tiles.shape
    stacked = step * CAP
    high = dot(unpack[: count * stacked], tiles.reshape(step * tile, lanes))
    return jnp.concatenate(
        [high[c * stacked : (c + 1) * stacked] for c in range(count)], axis=1
    ).astype(BF)


def kernel(
    n_group,
    n_dp,
    blk_hbm,
    prot_hbm,
    w_hbm,
    cot_hbm,
    table_hbm,
    hid_hbm,
    got_grad,
    dense_t_hbm,
    blk_ref,
    prot_ref,
    w_ref,
    cot_ref,
    table,
    hid,
    send_w,
    got_w,
    send_part,
    got_part,
    send_grad,
    dense,
    dense_t,
    pick,
    pick_t,
    sends,
    recvs,
    loads,
    stores,
):
    n = n_group * n_dp
    me = lax.axis_index("group") * n_dp + lax.axis_index("dp")
    pairs_of = [(blk_hbm, blk_ref), (prot_hbm, prot_ref), (w_hbm, w_ref)]
    others_of = [(table_hbm, table), (hid_hbm, hid), (cot_hbm, cot_ref)]
    copies = [
        pltpu.make_async_copy(a, b, loads.at[i]) for i, (a, b) in enumerate(pairs_of + others_of)
    ]
    for copy in copies:
        copy.start()
    load_pairs = copies[:3]
    load_table, load_hid, load_cot = copies[3:]

    def where_is(t):
        return (lax.div(t, n_dp), lax.rem(t, n_dp))

    barrier = pltpu.get_barrier_semaphore()

    def greet(i, carry):
        t = lax.rem(me + i, n)
        pl.semaphore_signal(barrier, inc=1, device_id=where_is(t), device_id_type=MESH)
        return carry

    lax.fori_loop(1, n, greet, 0)

    def exchange(send, got, phase):
        def start(i, carry):
            t = lax.rem(me + i, n)
            pltpu.make_async_remote_copy(
                src_ref=send.at[t],
                dst_ref=got.at[me],
                send_sem=sends.at[phase],
                recv_sem=recvs.at[phase],
                device_id=where_is(t),
                device_id_type=MESH,
            ).start()
            return carry

        lax.fori_loop(1, n, start, 0)

    others = pl.ds(0, n - 1)

    def arrived(got, phase):
        pltpu.make_async_copy(got.at[others], got.at[others], recvs.at[phase]).wait()

    def left(send, phase):
        pltpu.make_async_copy(send.at[others], send.at[others], sends.at[phase]).wait()

    width = table.shape[1]
    block_rows = w_ref.shape[1]
    blocks = table.shape[0] // block_rows
    chunks = width // LANES
    proteins = cot_ref.shape[0]
    pairs = w_ref.shape[0]
    tile = chunks * CAP
    slots = n * CAP
    step = min(TOGETHER, n)
    groups = n // step
    rows = step * tile
    few = groups <= 4

    def each(body):
        if few:
            for g in range(groups):
                body(g)
        else:
            lax.fori_loop(0, groups, lambda g, c: (body(g), c)[1], 0)

    def at(g, size):
        return pl.ds(g * size, size) if few else pl.ds(pl.multiple_of(g * size, size), size)

    for copy in load_pairs:
        copy.wait()
    blk = blk_ref[...]
    owner = lax.div(blk, blocks)
    local = lax.rem(blk, blocks)
    local_prot = prot_ref[...] - me * proteins
    square = (pairs, pairs)
    from_row, from_col = iota(square, 0), iota(square, 1)
    owner_f = owner.astype(F32)
    owner_col = jnp.sum(jnp.where(from_row == from_col, owner_f, 0.0), axis=1, keepdims=True)
    earlier = (owner_col == owner_f) & (from_row < from_col)
    rank = jnp.sum(jnp.where(earlier, 1.0, 0.0), axis=0, keepdims=True)
    slot = owner * CAP + rank.astype(jnp.int32)

    place_rows = iota((rows, pairs), 0)
    place_c = lax.rem(place_rows, tile) // CAP
    place_slot = (place_rows // tile) * CAP + lax.rem(place_rows, CAP)
    for_prot = ones_where(iota((chunks * PAD, pairs), 0) % PAD == local_prot)
    same_c = iota((chunks * PAD, rows), 0) // PAD == (iota((chunks * PAD, rows), 1) % tile) // CAP
    same_c_t = iota((rows, chunks * PAD), 1) // PAD == (iota((rows, chunks * PAD), 0) % tile) // CAP
    weights = w_ref[...]

    def place_of(g):
        return place_slot + g * (step * CAP) == slot

    def make_w(g):
        place = place_of(g) & (place_c == local)
        send_w[at(g, step)] = dot(ones_where(place), weights).astype(BF).reshape(step, tile, LANES)

    each(make_w)
    pl.semaphore_wait(barrier, n - 1)
    exchange(send_w, got_w, 0)
    got_w[me] = send_w[me]

    def make_pick(g):
        place = ones_where(place_of(g))
        pick[g] = jnp.where(same_c, dot_nt(for_prot, place), 0.0).astype(BF)
        pick_t[at(g, rows), :] = jnp.where(same_c_t, dot_nt(place, for_prot), 0.0).astype(BF)

    each(make_pick)

    stacked = step * CAP
    pack, unpack = repack(step, chunks)
    arrived(got_w, 0)

    def make_dense(g):
        dense[at(g, stacked), :] = unpacked(unpack, got_w[at(g, step)], blocks * block_rows // LANES)

    each(make_dense)
    load_table.wait()
    big = min(slots, 256)
    per_big = big // stacked

    def make_part(h):
        some = dense[pl.ds(h * big if few else pl.multiple_of(h * big, big), big), :]
        part = dot(some, table[...]).astype(BF)
        for j in range(per_big):
            own = part[j * stacked : (j + 1) * stacked]
            stack = jnp.concatenate(
                [own[:, c * LANES : (c + 1) * LANES] for c in range(chunks)], axis=0
            )
            send_part[at(h * per_big + j, step)] = (
                dot(pack, stack).astype(BF).reshape(step, tile, LANES)
            )

    if few:
        for h in range(slots // big):
            make_part(h)
    else:
        lax.fori_loop(0, slots // big, lambda h, c: (make_part(h), c)[1], 0)
    exchange(send_part, got_part, 1)
    got_part[me] = send_part[me]

    dense_t[...] = dense[...].astype(F32).T.astype(BF)
    store_dense = pltpu.make_async_copy(dense_t, dense_t_hbm, stores.at[0])
    store_dense.start()
    load_hid.wait()
    arrived(got_part, 1)

    def bag_of(g):
        return dot(pick[g], got_part[at(g, step)].reshape(rows, LANES))

    if few:
        stack = sum(bag_of(g) for g in range(groups))
    else:
        stack = lax.fori_loop(
            0, groups, lambda g, c: c + bag_of(g), jnp.zeros((chunks * PAD, LANES), F32)
        )
    bag = jnp.concatenate([stack[c * PAD : (c + 1) * PAD] for c in range(chunks)], axis=1)
    load_cot.wait()
    cot = cot_ref[...].astype(F32)
    cot = jnp.concatenate([cot, jnp.zeros((PAD - proteins, cot.shape[1]), F32)], axis=0)
    inv = lax.rsqrt(jnp.mean(bag * bag, axis=-1, keepdims=True) + 1e-06)
    unit = bag * inv
    pre = dot(unit.astype(BF), hid[...])
    sig = jax.nn.sigmoid(pre)
    dpre = (cot * sig * (1.0 + pre * (1.0 - sig))).astype(BF)
    dunit = dot_nt(dpre, hid[...])
    dbag = (dunit - unit * jnp.mean(dunit * unit, axis=-1, keepdims=True)) * inv
    dstack = jnp.concatenate(
        [dbag[:, c * LANES : (c + 1) * LANES] for c in range(chunks)], axis=0
    ).astype(BF)

    def make_grad(g):
        send_grad[at(g, step)] = (
            dot(pick_t[at(g, rows), :], dstack).astype(BF).reshape(step, tile, LANES)
        )

    each(make_grad)
    exchange(send_grad, got_grad, 2)
    own = pltpu.make_async_copy(send_grad.at[me], got_grad.at[me], stores.at[1])
    own.start()
    left(send_w, 0)
    left(send_part, 1)
    left(send_grad, 2)
    store_dense.wait()
    own.wait()
    arrived(got_grad, 2)


def update(
    dense_hbm,
    tiles_hbm,
    accum_hbm,
    table_hbm,
    out_hbm,
    acc_hbm,
    dense_t,
    tiles,
    accum,
    table,
    rows_out,
    acc_out,
    gathered,
    loads,
    stores,
):
    n, tile, _ = tiles.shape
    blocks, block_rows = accum.shape
    chunks = tile // CAP
    step = min(TOGETHER, n)
    groups = n // step
    stacked = step * CAP
    parts = [pl.ds(b * block_rows, block_rows) for b in range(blocks)]
    pairs_of = [(tiles_hbm, tiles), (dense_hbm, dense_t), (accum_hbm, accum)]
    pairs_of += [(table_hbm.at[some], table.at[some]) for some in parts]
    copies = [pltpu.make_async_copy(a, b, loads.at[i]) for i, (a, b) in enumerate(pairs_of)]
    for copy in copies:
        copy.start()
    _, unpack = repack(step, chunks)
    diagonal = iota((block_rows, block_rows), 0) == iota((block_rows, block_rows), 1)
    copies[0].wait()

    def make_gathered(g):
        few = groups <= 4
        gathered[pl.ds(g * stacked if few else pl.multiple_of(g * stacked, stacked), stacked), :] = (
            unpacked(unpack, tiles[pl.ds(g * step, step)], chunks)
        )

    if groups <= 4:
        for g in range(groups):
            make_gathered(g)
    else:
        lax.fori_loop(0, groups, lambda g, c: (make_gathered(g), c)[1], 0)
    copies[1].wait()
    copies[2].wait()
    writes = []
    for b, some in enumerate(parts):
        grad = dot(dense_t[some, :], gathered[...])
        mean = jnp.mean(grad * grad, axis=-1, keepdims=True)
        old = jnp.sum(jnp.where(diagonal, accum[b : b + 1, :], 0.0), axis=1, keepdims=True)
        new = old + mean
        scale = 0.3 / (jnp.sqrt(new) + 1e-08)
        copies[3 + b].wait()
        rows_out[some, :] = (table[some, :].astype(F32) - grad * scale).astype(BF)
        write = pltpu.make_async_copy(rows_out.at[some], out_hbm.at[some], stores.at[b])
        write.start()
        writes.append(write)
        acc_out[b : b + 1, :] = jnp.sum(jnp.where(diagonal, new, 0.0), axis=0, keepdims=True)
    write = pltpu.make_async_copy(acc_out, acc_hbm, stores.at[blocks])
    write.start()
    writes.append(write)
    for write in writes:
        write.wait()


def per_device(table, accum, pair_block, pair_protein, pair_weight, w_hidden, hidden_cot):
    n_group = lax.axis_size("group")
    n_dp = lax.axis_size("dp")
    n = n_group * n_dp
    rows_dev, width = table.shape
    pairs, block_rows = pair_weight.shape
    blocks = rows_dev // block_rows
    tile = (width // LANES) * CAP
    slots = n * CAP
    step = min(TOGETHER, n)
    hbm = pl.BlockSpec(memory_space=pl.ANY)
    tiles = pltpu.VMEM((n, tile, LANES), BF)
    stack = (width // LANES) * PAD
    got_grad, dense_t = pl.pallas_call(
        functools.partial(kernel, n_group, n_dp),
        out_shape=(
            jax.ShapeDtypeStruct((n, tile, LANES), BF),
            jax.ShapeDtypeStruct((rows_dev, slots), BF),
        ),
        in_specs=[hbm] * 6,
        out_specs=(hbm, hbm),
        scratch_shapes=[
            pltpu.VMEM((1, pairs), jnp.int32),
            pltpu.VMEM((1, pairs), jnp.int32),
            pltpu.VMEM(pair_weight.shape, BF),
            pltpu.VMEM(hidden_cot.shape, BF),
            pltpu.VMEM(table.shape, BF),
            pltpu.VMEM(w_hidden.shape, BF),
            tiles,
            tiles,
            tiles,
            tiles,
            tiles,
            pltpu.VMEM((slots, rows_dev), BF),
            pltpu.VMEM((rows_dev, slots), BF),
            pltpu.VMEM((n // step, stack, step * tile), BF),
            pltpu.VMEM((n * tile, stack), BF),
            pltpu.SemaphoreType.DMA((3,)),
            pltpu.SemaphoreType.DMA((3,)),
            pltpu.SemaphoreType.DMA((6,)),
            pltpu.SemaphoreType.DMA((2,)),
        ],
        compiler_params=pltpu.CompilerParams(
            collective_id=0, has_side_effects=True, vmem_limit_bytes=LIMIT
        ),
        name="bags",
    )(
        pair_block.reshape(1, pairs),
        pair_protein.reshape(1, pairs),
        pair_weight,
        hidden_cot,
        table,
        w_hidden,
    )
    new_table, new_accum = pl.pallas_call(
        update,
        out_shape=(
            jax.ShapeDtypeStruct(table.shape, BF),
            jax.ShapeDtypeStruct((blocks, block_rows), F32),
        ),
        in_specs=[hbm] * 4,
        out_specs=(hbm, hbm),
        scratch_shapes=[
            pltpu.VMEM((rows_dev, slots), BF),
            tiles,
            pltpu.VMEM((blocks, block_rows), F32),
            pltpu.VMEM(table.shape, BF),
            pltpu.VMEM(table.shape, BF),
            pltpu.VMEM((blocks, block_rows), F32),
            pltpu.VMEM((slots, width), BF),
            pltpu.SemaphoreType.DMA((3 + blocks,)),
            pltpu.SemaphoreType.DMA((1 + blocks,)),
        ],
        compiler_params=pltpu.CompilerParams(vmem_limit_bytes=LIMIT),
        name="update",
    )(dense_t, got_grad, accum.reshape(blocks, block_rows), table)
    return new_table, new_accum.reshape(rows_dev)


def solution(mesh):
    in_specs = (
        P(("group", "dp"), None),
        P(("group", "dp")),
        P(("group", "dp")),
        P(("group", "dp")),
        P(("group", "dp"), None),
        P(),
        P(("group", "dp"), None),
    )
    out_specs = (P(("group", "dp"), None), P(("group", "dp")))
    return jax.shard_map(
        per_device, mesh=mesh, in_specs=in_specs, out_specs=out_specs, check_vma=False
    )
```

```python
import functools

import jax
import jax.numpy as jnp
from jax import lax
from jax.experimental import pallas as pl
from jax.experimental.pallas import tpu as pltpu
from jax.sharding import PartitionSpec as P

CAP = 2
LANES = 128
TOGETHER = 16
PAD = 8
LIMIT = 40 * 1024 * 1024
MESH = pl.DeviceIdType.MESH
BF = jnp.bfloat16
F32 = jnp.float32


def dot(a, b):
    return jnp.dot(a, b, preferred_element_type=F32)


def dot_nt(a, b):
    return lax.dot_general(a, b, (((1,), (1,)), ((), ())), preferred_element_type=F32)


def iota(shape, dim):
    return lax.broadcasted_iota(jnp.int32, shape, dim)


def ones_where(mask):
    return jnp.where(mask, 1.0, 0.0).astype(BF)


def repack(step, chunks):
    tile, stacked = chunks * CAP, step * CAP
    shape = (step * tile, step * tile)
    to_r, to_c = iota(shape, 0), iota(shape, 1)
    r_c, r_d, r_k = to_r // stacked, (to_r % stacked) // CAP, to_r % CAP
    unpack = ones_where(to_c == r_d * tile + r_c * CAP + r_k)
    t_c, t_d, t_k = to_c // stacked, (to_c % stacked) // CAP, to_c % CAP
    pack = ones_where(to_r == t_d * tile + t_c * CAP + t_k)
    return pack, unpack


def unpacked(unpack, tiles, count):
    step, tile, lanes = tiles.shape
    stacked = step * CAP
    high = dot(unpack[: count * stacked], tiles.reshape(step * tile, lanes))
    return jnp.concatenate(
        [high[c * stacked : (c + 1) * stacked] for c in range(count)], axis=1
    ).astype(BF)


def kernel(
    n_group,
    n_dp,
    blk_hbm,
    prot_hbm,
    w_hbm,
    cot_hbm,
    accum_hbm,
    table_hbm,
    hid_hbm,
    got_grad,
    dense_t,
    accum,
    table,
    blk_ref,
    prot_ref,
    w_ref,
    cot_ref,
    hid,
    send_w,
    got_w,
    send_part,
    got_part,
    send_grad,
    dense,
    pick,
    pick_t,
    sends,
    recvs,
    loads,
):
    n = n_group * n_dp
    mine = (lax.axis_index("group"), lax.axis_index("dp"))
    me = mine[0] * n_dp + mine[1]
    pairs_of = [(blk_hbm, blk_ref), (prot_hbm, prot_ref), (w_hbm, w_ref)]
    others_of = [(table_hbm, table), (hid_hbm, hid), (cot_hbm, cot_ref), (accum_hbm, accum)]
    copies = [
        pltpu.make_async_copy(a, b, loads.at[i]) for i, (a, b) in enumerate(pairs_of + others_of)
    ]
    for copy in copies:
        copy.start()
    load_pairs = copies[:3]
    load_table, load_hid, load_cot, load_accum = copies[3:]

    def to_all(act):
        if n <= 32:
            at_group = [lax.rem(mine[0] + a, n_group) for a in range(n_group)]
            at_dp = [lax.rem(mine[1] + b, n_dp) for b in range(n_dp)]
            for b in sorted(range(n_dp), key=lambda b: -min(b, n_dp - b)):
                for a in range(n_group):
                    if a or b:
                        act((at_group[a], at_dp[b]), at_group[a] * n_dp + at_dp[b])
        else:

            def one(i, carry):
                t = lax.rem(me + i, n)
                act((lax.div(t, n_dp), lax.rem(t, n_dp)), t)
                return carry

            lax.fori_loop(1, n, one, 0)

    barrier = pltpu.get_barrier_semaphore()
    to_all(
        lambda device, t: pl.semaphore_signal(
            barrier, inc=1, device_id=device, device_id_type=MESH
        )
    )

    def exchange(send, got, phase):
        to_all(
            lambda device, t: pltpu.make_async_remote_copy(
                src_ref=send.at[t],
                dst_ref=got.at[me],
                send_sem=sends.at[phase],
                recv_sem=recvs.at[phase],
                device_id=device,
                device_id_type=MESH,
            ).start()
        )
        got[me] = send[me]

    others = pl.ds(0, n - 1)

    def arrived(got, phase):
        pltpu.make_async_copy(got.at[others], got.at[others], recvs.at[phase]).wait()

    def left(send, phase):
        pltpu.make_async_copy(send.at[others], send.at[others], sends.at[phase]).wait()

    width = table.shape[1]
    block_rows = w_ref.shape[1]
    blocks = table.shape[0] // block_rows
    chunks = width // LANES
    proteins = cot_ref.shape[0]
    pairs = w_ref.shape[0]
    tile = chunks * CAP
    slots = n * CAP
    step = min(TOGETHER, n)
    groups = n // step
    rows = step * tile
    few = groups <= 4

    def each(body):
        if few:
            for g in range(groups):
                body(g)
        else:
            lax.fori_loop(0, groups, lambda g, c: (body(g), c)[1], 0)

    def at(g, size):
        return pl.ds(g * size, size) if few else pl.ds(pl.multiple_of(g * size, size), size)

    for copy in load_pairs:
        copy.wait()
    blk = blk_ref[...]
    owner = lax.div(blk, blocks)
    local = lax.rem(blk, blocks)
    local_prot = prot_ref[...] - me * proteins
    square = (pairs, pairs)
    from_row, from_col = iota(square, 0), iota(square, 1)
    owner_f = owner.astype(F32)
    owner_col = jnp.sum(jnp.where(from_row == from_col, owner_f, 0.0), axis=1, keepdims=True)
    earlier = (owner_col == owner_f) & (from_row < from_col)
    rank = jnp.sum(jnp.where(earlier, 1.0, 0.0), axis=0, keepdims=True)
    slot = owner * CAP + rank.astype(jnp.int32)

    place_rows = iota((rows, pairs), 0)
    place_c = lax.rem(place_rows, tile) // CAP
    place_slot = (place_rows // tile) * CAP + lax.rem(place_rows, CAP)
    for_prot = ones_where(iota((chunks * PAD, pairs), 0) % PAD == local_prot)
    same_c = iota((chunks * PAD, rows), 0) // PAD == (iota((chunks * PAD, rows), 1) % tile) // CAP
    same_c_t = iota((rows, chunks * PAD), 1) // PAD == (iota((rows, chunks * PAD), 0) % tile) // CAP
    weights = w_ref[...]

    def place_of(g):
        return place_slot + g * (step * CAP) == slot

    def make_w(g):
        place = place_of(g) & (place_c == local)
        send_w[at(g, step)] = dot(ones_where(place), weights).astype(BF).reshape(step, tile, LANES)

    each(make_w)
    pl.semaphore_wait(barrier, n - 1)
    exchange(send_w, got_w, 0)

    def make_pick(g):
        place = ones_where(place_of(g))
        pick[g] = jnp.where(same_c, dot_nt(for_prot, place), 0.0).astype(BF)
        pick_t[at(g, rows), :] = jnp.where(same_c_t, dot_nt(place, for_prot), 0.0).astype(BF)

    each(make_pick)

    stacked = step * CAP
    pack, unpack = repack(step, chunks)
    arrived(got_w, 0)

    def make_dense(g):
        dense[at(g, stacked), :] = unpacked(unpack, got_w[at(g, step)], blocks * block_rows // LANES)

    each(make_dense)
    load_table.wait()
    big = min(slots, 256)
    per_big = big // stacked

    def make_part(h):
        some = dense[pl.ds(h * big if few else pl.multiple_of(h * big, big), big), :]
        part = dot(some, table[...]).astype(BF)
        for j in range(per_big):
            own = part[j * stacked : (j + 1) * stacked]
            stack = jnp.concatenate(
                [own[:, c * LANES : (c + 1) * LANES] for c in range(chunks)], axis=0
            )
            send_part[at(h * per_big + j, step)] = (
                dot(pack, stack).astype(BF).reshape(step, tile, LANES)
            )

    if few:
        for h in range(slots // big):
            make_part(h)
    else:
        lax.fori_loop(0, slots // big, lambda h, c: (make_part(h), c)[1], 0)
    exchange(send_part, got_part, 1)

    dense_t[...] = dense[...].astype(F32).T.astype(BF)
    load_accum.wait()
    load_hid.wait()
    arrived(got_part, 1)

    def bag_of(g):
        return dot(pick[g], got_part[at(g, step)].reshape(rows, LANES))

    if few:
        stack = sum(bag_of(g) for g in range(groups))
    else:
        stack = lax.fori_loop(
            0, groups, lambda g, c: c + bag_of(g), jnp.zeros((chunks * PAD, LANES), F32)
        )
    bag = jnp.concatenate([stack[c * PAD : (c + 1) * PAD] for c in range(chunks)], axis=1)
    load_cot.wait()
    cot = cot_ref[...].astype(F32)
    cot = jnp.concatenate([cot, jnp.zeros((PAD - proteins, cot.shape[1]), F32)], axis=0)
    inv = lax.rsqrt(jnp.mean(bag * bag, axis=-1, keepdims=True) + 1e-06)
    unit = bag * inv
    pre = dot(unit.astype(BF), hid[...])
    sig = jax.nn.sigmoid(pre)
    dpre = (cot * sig * (1.0 + pre * (1.0 - sig))).astype(BF)
    dunit = dot_nt(dpre, hid[...])
    dbag = (dunit - unit * jnp.mean(dunit * unit, axis=-1, keepdims=True)) * inv
    dstack = jnp.concatenate(
        [dbag[:, c * LANES : (c + 1) * LANES] for c in range(chunks)], axis=0
    ).astype(BF)

    def make_grad(g):
        send_grad[at(g, step)] = (
            dot(pick_t[at(g, rows), :], dstack).astype(BF).reshape(step, tile, LANES)
        )

    each(make_grad)
    exchange(send_grad, got_grad, 2)
    left(send_w, 0)
    left(send_part, 1)
    left(send_grad, 2)
    arrived(got_grad, 2)


def update(dense_t, tiles, accum, table, out_hbm, acc_hbm, rows_out, acc_out, gathered, stores):
    n, tile, _ = tiles.shape
    blocks, block_rows = accum.shape
    chunks = tile // CAP
    step = min(TOGETHER, n)
    groups = n // step
    stacked = step * CAP
    parts = [pl.ds(b * block_rows, block_rows) for b in range(blocks)]
    _, unpack = repack(step, chunks)
    diagonal = iota((block_rows, block_rows), 0) == iota((block_rows, block_rows), 1)

    def make_gathered(g):
        few = groups <= 4
        gathered[pl.ds(g * stacked if few else pl.multiple_of(g * stacked, stacked), stacked), :] = (
            unpacked(unpack, tiles[pl.ds(g * step, step)], chunks)
        )

    if groups <= 4:
        for g in range(groups):
            make_gathered(g)
    else:
        lax.fori_loop(0, groups, lambda g, c: (make_gathered(g), c)[1], 0)
    writes = []
    for b, some in enumerate(parts):
        grad = dot(dense_t[some, :], gathered[...])
        mean = jnp.mean(grad * grad, axis=-1, keepdims=True)
        old = jnp.sum(jnp.where(diagonal, accum[b : b + 1, :], 0.0), axis=1, keepdims=True)
        new = old + mean
        scale = 0.3 / (jnp.sqrt(new) + 1e-08)
        rows_out[some, :] = (table[some, :].astype(F32) - grad * scale).astype(BF)
        write = pltpu.make_async_copy(rows_out.at[some], out_hbm.at[some], stores.at[b])
        write.start()
        writes.append(write)
        acc_out[b : b + 1, :] = jnp.sum(jnp.where(diagonal, new, 0.0), axis=0, keepdims=True)
    write = pltpu.make_async_copy(acc_out, acc_hbm, stores.at[blocks])
    write.start()
    writes.append(write)
    for write in writes:
        write.wait()


def per_device(table, accum, pair_block, pair_protein, pair_weight, w_hidden, hidden_cot):
    n_group = lax.axis_size("group")
    n_dp = lax.axis_size("dp")
    n = n_group * n_dp
    rows_dev, width = table.shape
    pairs, block_rows = pair_weight.shape
    blocks = rows_dev // block_rows
    tile = (width // LANES) * CAP
    slots = n * CAP
    step = min(TOGETHER, n)
    hbm = pl.BlockSpec(memory_space=pltpu.HBM)
    vmem = pl.BlockSpec(memory_space=pltpu.VMEM)
    tiles = pltpu.VMEM((n, tile, LANES), BF)
    stack = (width // LANES) * PAD
    got_grad, dense_t, accum_held, table_held = pl.pallas_call(
        functools.partial(kernel, n_group, n_dp),
        out_shape=(
            jax.ShapeDtypeStruct((n, tile, LANES), BF),
            jax.ShapeDtypeStruct((rows_dev, slots), BF),
            jax.ShapeDtypeStruct((blocks, block_rows), F32),
            jax.ShapeDtypeStruct(table.shape, BF),
        ),
        in_specs=[hbm] * 7,
        out_specs=(vmem,) * 4,
        scratch_shapes=[
            pltpu.VMEM((1, pairs), jnp.int32),
            pltpu.VMEM((1, pairs), jnp.int32),
            pltpu.VMEM(pair_weight.shape, BF),
            pltpu.VMEM(hidden_cot.shape, BF),
            pltpu.VMEM(w_hidden.shape, BF),
            tiles,
            tiles,
            tiles,
            tiles,
            tiles,
            pltpu.VMEM((slots, rows_dev), BF),
            pltpu.VMEM((n // step, stack, step * tile), BF),
            pltpu.VMEM((n * tile, stack), BF),
            pltpu.SemaphoreType.DMA((3,)),
            pltpu.SemaphoreType.DMA((3,)),
            pltpu.SemaphoreType.DMA((7,)),
        ],
        compiler_params=pltpu.CompilerParams(
            collective_id=0, has_side_effects=True, vmem_limit_bytes=LIMIT
        ),
        name="bags",
    )(
        *(
            pltpu.with_memory_space_constraint(x, pltpu.HBM)
            for x in (
                pair_block.reshape(1, pairs),
                pair_protein.reshape(1, pairs),
                pair_weight,
                hidden_cot,
                accum.reshape(blocks, block_rows),
                table,
                w_hidden,
            )
        )
    )
    new_table, new_accum = pl.pallas_call(
        update,
        out_shape=(
            jax.ShapeDtypeStruct(table.shape, BF),
            jax.ShapeDtypeStruct((blocks, block_rows), F32),
        ),
        in_specs=[vmem] * 4,
        out_specs=(hbm, hbm),
        scratch_shapes=[
            pltpu.VMEM(table.shape, BF),
            pltpu.VMEM((blocks, block_rows), F32),
            pltpu.VMEM((slots, width), BF),
            pltpu.SemaphoreType.DMA((1 + blocks,)),
        ],
        compiler_params=pltpu.CompilerParams(vmem_limit_bytes=LIMIT // 2),
        name="update",
    )(dense_t, got_grad, accum_held, table_held)
    return new_table, new_accum.reshape(rows_dev)


def solution(mesh):
    in_specs = (
        P(("group", "dp"), None),
        P(("group", "dp")),
        P(("group", "dp")),
        P(("group", "dp")),
        P(("group", "dp"), None),
        P(),
        P(("group", "dp"), None),
    )
    out_specs = (P(("group", "dp"), None), P(("group", "dp")))
    return jax.shard_map(
        per_device, mesh=mesh, in_specs=in_specs, out_specs=out_specs, check_vma=False
    )
```

```python
import functools

import jax
import jax.numpy as jnp
from jax import lax
from jax.experimental import pallas as pl
from jax.experimental.pallas import tpu as pltpu
from jax.sharding import PartitionSpec as P

CAP = 2
LANES = 128
TOGETHER = 16
PAD = 8
MARK = 2.0**-15
LIMIT = 40 * 1024 * 1024
MESH = pl.DeviceIdType.MESH
BF = jnp.bfloat16
F32 = jnp.float32


def dot(a, b):
    return jnp.dot(a, b, preferred_element_type=F32)


def dot_nt(a, b):
    return lax.dot_general(a, b, (((1,), (1,)), ((), ())), preferred_element_type=F32)


def iota(shape, dim):
    return lax.broadcasted_iota(jnp.int32, shape, dim)


def over(x, k):
    return jnp.right_shift(x, k.bit_length() - 1)


def rest(x, k):
    return jnp.bitwise_and(x, k - 1)


def ones_where(mask):
    return jnp.where(mask, 1.0, 0.0).astype(BF)


def repack(step, chunks):
    tile, stacked = chunks * CAP, step * CAP
    shape = (step * tile, step * tile)
    to_r, to_c = iota(shape, 0), iota(shape, 1)
    r_c, r_d, r_k = over(to_r, stacked), over(rest(to_r, stacked), CAP), rest(to_r, CAP)
    unpack = ones_where(to_c == r_d * tile + r_c * CAP + r_k)
    t_c, t_d, t_k = over(to_c, stacked), over(rest(to_c, stacked), CAP), rest(to_c, CAP)
    pack = ones_where(to_r == t_d * tile + t_c * CAP + t_k)
    return pack, unpack


def unpacked(unpack, tiles, count):
    step, tile, lanes = tiles.shape
    stacked = step * CAP
    high = dot(unpack[: count * stacked], tiles.reshape(step * tile, lanes))
    return jnp.concatenate(
        [high[c * stacked : (c + 1) * stacked] for c in range(count)], axis=1
    ).astype(BF)


def kernel(
    n_group,
    n_dp,
    blk_hbm,
    prot_hbm,
    w_hbm,
    cot_hbm,
    accum_hbm,
    table_hbm,
    hid_hbm,
    got_grad,
    dense_t,
    accum,
    table,
    blk_ref,
    prot_ref,
    w_ref,
    cot_ref,
    hid,
    send_w,
    got_w,
    send_part,
    got_part,
    send_grad,
    dense,
    pick,
    pick_t,
    sends,
    recvs,
    loads,
):
    n = n_group * n_dp
    mine = (lax.axis_index("group"), lax.axis_index("dp"))
    me = mine[0] * n_dp + mine[1]
    pairs_of = [(blk_hbm, blk_ref), (prot_hbm, prot_ref), (w_hbm, w_ref)]
    others_of = [(table_hbm, table), (hid_hbm, hid), (cot_hbm, cot_ref), (accum_hbm, accum)]
    copies = [
        pltpu.make_async_copy(a, b, loads.at[i]) for i, (a, b) in enumerate(pairs_of + others_of)
    ]
    for copy in copies:
        copy.start()
    load_pairs = copies[:3]
    load_table, load_hid, load_cot, load_accum = copies[3:]

    def to_all(act):
        if n <= 32:
            at_group = [lax.rem(mine[0] + a, n_group) for a in range(n_group)]
            at_dp = [lax.rem(mine[1] + b, n_dp) for b in range(n_dp)]
            for b in sorted(range(n_dp), key=lambda b: -min(b, n_dp - b)):
                for a in range(n_group):
                    if a or b:
                        act((at_group[a], at_dp[b]), at_group[a] * n_dp + at_dp[b])
        else:

            def one(i, carry):
                t = lax.rem(me + i, n)
                act((lax.div(t, n_dp), lax.rem(t, n_dp)), t)
                return carry

            lax.fori_loop(1, n, one, 0)

    barrier = pltpu.get_barrier_semaphore()
    to_all(
        lambda device, t: pl.semaphore_signal(
            barrier, inc=1, device_id=device, device_id_type=MESH
        )
    )

    def exchange(send, got, phase):
        to_all(
            lambda device, t: pltpu.make_async_remote_copy(
                src_ref=send.at[t],
                dst_ref=got.at[me],
                send_sem=sends.at[phase],
                recv_sem=recvs.at[phase],
                device_id=device,
                device_id_type=MESH,
            ).start()
        )
        got[me] = send[me]

    others = pl.ds(0, n - 1)

    def arrived(got, phase):
        pltpu.make_async_copy(got.at[others], got.at[others], recvs.at[phase]).wait()

    def left(send, phase):
        pltpu.make_async_copy(send.at[others], send.at[others], sends.at[phase]).wait()

    width = table.shape[1]
    block_rows = w_ref.shape[1]
    blocks = table.shape[0] // block_rows
    chunks = width // LANES
    proteins = cot_ref.shape[0]
    pairs = w_ref.shape[0]
    tile = chunks * CAP
    slots = n * CAP
    step = min(TOGETHER, n)
    groups = n // step
    rows = step * tile
    few = groups <= 4

    def each(body):
        if few:
            for g in range(groups):
                body(g)
        else:
            lax.fori_loop(0, groups, lambda g, c: (body(g), c)[1], 0)

    def at(g, size):
        return pl.ds(g * size, size) if few else pl.ds(pl.multiple_of(g * size, size), size)

    for copy in load_pairs:
        copy.wait()
    blk = blk_ref[...]
    owner = over(blk, blocks)
    local = rest(blk, blocks)
    local_prot = prot_ref[...] - me * proteins
    square = (pairs, pairs)
    from_row, from_col = iota(square, 0), iota(square, 1)
    owner_f = owner.astype(F32)
    owner_col = jnp.sum(jnp.where(from_row == from_col, owner_f, 0.0), axis=1, keepdims=True)
    earlier = (owner_col == owner_f) & (from_row < from_col)
    rank = jnp.sum(jnp.where(earlier, 1.0, 0.0), axis=0, keepdims=True)
    slot = owner * CAP + rank.astype(jnp.int32)

    place_rows = iota((rows, pairs), 0)
    place_slot = over(place_rows, tile) * CAP + rest(place_rows, CAP)
    weights = w_ref[...]

    def place_of(g):
        return place_slot + g * (step * CAP) == slot

    slot_rows = iota((step * CAP, pairs), 0)

    def make_w(g):
        place = slot_rows + g * (step * CAP) == slot
        block = jnp.sum(jnp.where(place, local.astype(F32), 0.0), axis=1, keepdims=True)
        marked = dot(ones_where(place), weights) * (1.0 + block * MARK)
        send_w[at(g, step)] = marked.reshape(step, CAP, block_rows)

    each(make_w)
    pl.semaphore_wait(barrier, n - 1)
    exchange(send_w, got_w, 0)

    for_prot = ones_where(rest(iota((chunks * PAD, pairs), 0), PAD) == local_prot)
    shape = (chunks * PAD, rows)
    same_c = over(iota(shape, 0), PAD) == over(rest(iota(shape, 1), tile), CAP)
    shape = (rows, chunks * PAD)
    same_c_t = over(iota(shape, 1), PAD) == over(rest(iota(shape, 0), tile), CAP)

    def make_pick(g):
        place = ones_where(place_of(g))
        pick[g] = jnp.where(same_c, dot_nt(for_prot, place), 0.0).astype(BF)
        pick_t[at(g, rows), :] = jnp.where(same_c_t, dot_nt(place, for_prot), 0.0).astype(BF)

    each(make_pick)

    stacked = step * CAP
    pack, _ = repack(step, chunks)
    arrived(got_w, 0)

    def make_dense(g):
        marked = got_w[at(g, step)].reshape(stacked, block_rows)
        plain = marked.astype(BF).astype(F32)
        dense[at(g, stacked), :] = jnp.concatenate(
            [jnp.where(marked == plain * (1.0 + b * MARK), plain, 0.0) for b in range(blocks)],
            axis=1,
        ).astype(BF)

    each(make_dense)
    load_table.wait()
    big = min(slots, 256)
    per_big = big // stacked

    def make_part(h):
        some = dense[pl.ds(h * big if few else pl.multiple_of(h * big, big), big), :]
        part = dot(some, table[...]).astype(BF)
        for j in range(per_big):
            own = part[j * stacked : (j + 1) * stacked]
            stack = jnp.concatenate(
                [own[:, c * LANES : (c + 1) * LANES] for c in range(chunks)], axis=0
            )
            send_part[at(h * per_big + j, step)] = (
                dot(pack, stack).astype(BF).reshape(step, tile, LANES)
            )

    if few:
        for h in range(slots // big):
            make_part(h)
    else:
        lax.fori_loop(0, slots // big, lambda h, c: (make_part(h), c)[1], 0)
    exchange(send_part, got_part, 1)

    dense_t[...] = dense[...].astype(F32).T.astype(BF)
    load_accum.wait()
    load_hid.wait()
    arrived(got_part, 1)

    def bag_of(g):
        return dot(pick[g], got_part[at(g, step)].reshape(rows, LANES))

    if few:
        stack = sum(bag_of(g) for g in range(groups))
    else:
        stack = lax.fori_loop(
            0, groups, lambda g, c: c + bag_of(g), jnp.zeros((chunks * PAD, LANES), F32)
        )
    bag = jnp.concatenate([stack[c * PAD : (c + 1) * PAD] for c in range(chunks)], axis=1)
    load_cot.wait()
    cot = cot_ref[...].astype(F32)
    cot = jnp.concatenate([cot, jnp.zeros((PAD - proteins, cot.shape[1]), F32)], axis=0)
    inv = lax.rsqrt(jnp.mean(bag * bag, axis=-1, keepdims=True) + 1e-06)
    unit = bag * inv
    pre = dot(unit.astype(BF), hid[...])
    sig = jax.nn.sigmoid(pre)
    dpre = (cot * sig * (1.0 + pre * (1.0 - sig))).astype(BF)
    dunit = dot_nt(dpre, hid[...])
    dbag = (dunit - unit * jnp.mean(dunit * unit, axis=-1, keepdims=True)) * inv
    dstack = jnp.concatenate(
        [dbag[:, c * LANES : (c + 1) * LANES] for c in range(chunks)], axis=0
    ).astype(BF)

    def make_grad(g):
        send_grad[at(g, step)] = (
            dot(pick_t[at(g, rows), :], dstack).astype(BF).reshape(step, tile, LANES)
        )

    each(make_grad)
    exchange(send_grad, got_grad, 2)
    left(send_w, 0)
    left(send_part, 1)
    left(send_grad, 2)
    arrived(got_grad, 2)


def update(dense_t, tiles, accum, table, out_hbm, acc_hbm, rows_out, acc_out, gathered, stores):
    n, tile, _ = tiles.shape
    blocks, block_rows = accum.shape
    chunks = tile // CAP
    step = min(TOGETHER, n)
    groups = n // step
    stacked = step * CAP
    parts = [pl.ds(b * block_rows, block_rows) for b in range(blocks)]
    _, unpack = repack(step, chunks)
    diagonal = iota((block_rows, block_rows), 0) == iota((block_rows, block_rows), 1)

    def make_gathered(g):
        few = groups <= 4
        gathered[pl.ds(g * stacked if few else pl.multiple_of(g * stacked, stacked), stacked), :] = (
            unpacked(unpack, tiles[pl.ds(g * step, step)], chunks)
        )

    if groups <= 4:
        for g in range(groups):
            make_gathered(g)
    else:
        lax.fori_loop(0, groups, lambda g, c: (make_gathered(g), c)[1], 0)
    writes = []
    for b, some in enumerate(parts):
        grad = dot(dense_t[some, :], gathered[...])
        mean = jnp.mean(grad * grad, axis=-1, keepdims=True)
        old = jnp.sum(jnp.where(diagonal, accum[b : b + 1, :], 0.0), axis=1, keepdims=True)
        new = old + mean
        scale = 0.3 / (jnp.sqrt(new) + 1e-08)
        rows_out[some, :] = (table[some, :].astype(F32) - grad * scale).astype(BF)
        write = pltpu.make_async_copy(rows_out.at[some], out_hbm.at[some], stores.at[b])
        write.start()
        writes.append(write)
        acc_out[b : b + 1, :] = jnp.sum(jnp.where(diagonal, new, 0.0), axis=0, keepdims=True)
    write = pltpu.make_async_copy(acc_out, acc_hbm, stores.at[blocks])
    write.start()
    writes.append(write)
    for write in writes:
        write.wait()


def per_device(table, accum, pair_block, pair_protein, pair_weight, w_hidden, hidden_cot):
    n_group = lax.axis_size("group")
    n_dp = lax.axis_size("dp")
    n = n_group * n_dp
    rows_dev, width = table.shape
    pairs, block_rows = pair_weight.shape
    blocks = rows_dev // block_rows
    tile = (width // LANES) * CAP
    slots = n * CAP
    step = min(TOGETHER, n)
    hbm = pl.BlockSpec(memory_space=pltpu.HBM)
    vmem = pl.BlockSpec(memory_space=pltpu.VMEM)
    tiles = pltpu.VMEM((n, tile, LANES), BF)
    stack = (width // LANES) * PAD
    got_grad, dense_t, accum_held, table_held = pl.pallas_call(
        functools.partial(kernel, n_group, n_dp),
        out_shape=(
            jax.ShapeDtypeStruct((n, tile, LANES), BF),
            jax.ShapeDtypeStruct((rows_dev, slots), BF),
            jax.ShapeDtypeStruct((blocks, block_rows), F32),
            jax.ShapeDtypeStruct(table.shape, BF),
        ),
        in_specs=[hbm] * 7,
        out_specs=(vmem,) * 4,
        scratch_shapes=[
            pltpu.VMEM((1, pairs), jnp.int32),
            pltpu.VMEM((1, pairs), jnp.int32),
            pltpu.VMEM(pair_weight.shape, BF),
            pltpu.VMEM(hidden_cot.shape, BF),
            pltpu.VMEM(w_hidden.shape, BF),
            pltpu.VMEM((n, CAP, block_rows), F32),
            pltpu.VMEM((n, CAP, block_rows), F32),
            tiles,
            tiles,
            tiles,
            pltpu.VMEM((slots, rows_dev), BF),
            pltpu.VMEM((n // step, stack, step * tile), BF),
            pltpu.VMEM((n * tile, stack), BF),
            pltpu.SemaphoreType.DMA((3,)),
            pltpu.SemaphoreType.DMA((3,)),
            pltpu.SemaphoreType.DMA((7,)),
        ],
        compiler_params=pltpu.CompilerParams(
            collective_id=0, has_side_effects=True, vmem_limit_bytes=LIMIT
        ),
        name="bags",
    )(
        *(
            pltpu.with_memory_space_constraint(x, pltpu.HBM)
            for x in (
                pair_block.reshape(1, pairs),
                pair_protein.reshape(1, pairs),
                pair_weight,
                hidden_cot,
                accum.reshape(blocks, block_rows),
                table,
                w_hidden,
            )
        )
    )
    new_table, new_accum = pl.pallas_call(
        update,
        out_shape=(
            jax.ShapeDtypeStruct(table.shape, BF),
            jax.ShapeDtypeStruct((blocks, block_rows), F32),
        ),
        in_specs=[vmem] * 4,
        out_specs=(hbm, hbm),
        scratch_shapes=[
            pltpu.VMEM(table.shape, BF),
            pltpu.VMEM((blocks, block_rows), F32),
            pltpu.VMEM((slots, width), BF),
            pltpu.SemaphoreType.DMA((1 + blocks,)),
        ],
        compiler_params=pltpu.CompilerParams(vmem_limit_bytes=LIMIT // 2),
        name="update",
    )(dense_t, got_grad, accum_held, table_held)
    return new_table, new_accum.reshape(rows_dev)


def solution(mesh):
    in_specs = (
        P(("group", "dp"), None),
        P(("group", "dp")),
        P(("group", "dp")),
        P(("group", "dp")),
        P(("group", "dp"), None),
        P(),
        P(("group", "dp"), None),
    )
    out_specs = (P(("group", "dp"), None), P(("group", "dp")))
    return jax.shard_map(
        per_device, mesh=mesh, in_specs=in_specs, out_specs=out_specs, check_vma=False
    )
```

```python
import functools

import jax
import jax.numpy as jnp
from jax import lax
from jax.experimental import pallas as pl
from jax.experimental.pallas import tpu as pltpu
from jax.sharding import PartitionSpec as P

CAP = 2
LANES = 128
TOGETHER = 16
PAD = 8
MARK = 2.0**-15
LIMIT = 40 * 1024 * 1024
MESH = pl.DeviceIdType.MESH
BF = jnp.bfloat16
F32 = jnp.float32


def dot(a, b):
    return jnp.dot(a, b, preferred_element_type=F32)


def dot_nt(a, b):
    return lax.dot_general(a, b, (((1,), (1,)), ((), ())), preferred_element_type=F32)


def iota(shape, dim):
    return lax.broadcasted_iota(jnp.int32, shape, dim)


def over(x, k):
    return jnp.right_shift(x, k.bit_length() - 1)


def rest(x, k):
    return jnp.bitwise_and(x, k - 1)


def ones_where(mask):
    return jnp.where(mask, 1.0, 0.0).astype(BF)


def repack(step, chunks):
    tile, stacked = chunks * CAP, step * CAP
    shape = (step * tile, step * tile)
    to_r, to_c = iota(shape, 0), iota(shape, 1)
    r_c, r_d, r_k = over(to_r, stacked), over(rest(to_r, stacked), CAP), rest(to_r, CAP)
    unpack = ones_where(to_c == r_d * tile + r_c * CAP + r_k)
    t_c, t_d, t_k = over(to_c, stacked), over(rest(to_c, stacked), CAP), rest(to_c, CAP)
    pack = ones_where(to_r == t_d * tile + t_c * CAP + t_k)
    return pack, unpack


def unpacked(unpack, tiles, count):
    step, tile, lanes = tiles.shape
    stacked = step * CAP
    high = dot(unpack[: count * stacked], tiles.reshape(step * tile, lanes))
    return jnp.concatenate(
        [high[c * stacked : (c + 1) * stacked] for c in range(count)], axis=1
    ).astype(BF)


def kernel(
    n_group,
    n_dp,
    blk_hbm,
    prot_hbm,
    w_hbm,
    cot_hbm,
    accum_hbm,
    table_hbm,
    hid_hbm,
    got_grad,
    dense_t,
    accum,
    table,
    blk_ref,
    prot_ref,
    w_ref,
    cot_ref,
    hid,
    hid_t,
    send_w,
    got_w,
    send_part,
    got_part,
    send_grad,
    dense,
    pick,
    pick_t,
    sends,
    recvs,
    loads,
):
    n = n_group * n_dp
    mine = (lax.axis_index("group"), lax.axis_index("dp"))
    me = mine[0] * n_dp + mine[1]
    pairs_of = [(blk_hbm, blk_ref), (prot_hbm, prot_ref), (w_hbm, w_ref)]
    others_of = [(table_hbm, table), (hid_hbm, hid), (cot_hbm, cot_ref), (accum_hbm, accum)]
    copies = [
        pltpu.make_async_copy(a, b, loads.at[i]) for i, (a, b) in enumerate(pairs_of + others_of)
    ]
    for copy in copies:
        copy.start()
    load_pairs = copies[:3]
    load_table, load_hid, load_cot, load_accum = copies[3:]

    def to_all(act):
        if n <= 32:
            at_group = [lax.rem(mine[0] + a, n_group) for a in range(n_group)]
            at_dp = [lax.rem(mine[1] + b, n_dp) for b in range(n_dp)]
            for b in sorted(range(n_dp), key=lambda b: -min(b, n_dp - b)):
                for a in range(n_group):
                    if a or b:
                        act((at_group[a], at_dp[b]), at_group[a] * n_dp + at_dp[b])
        else:

            def one(i, carry):
                t = lax.rem(me + i, n)
                act((lax.div(t, n_dp), lax.rem(t, n_dp)), t)
                return carry

            lax.fori_loop(1, n, one, 0)

    barrier = pltpu.get_barrier_semaphore()
    to_all(
        lambda device, t: pl.semaphore_signal(
            barrier, inc=1, device_id=device, device_id_type=MESH
        )
    )

    def exchange(send, got, phase):
        to_all(
            lambda device, t: pltpu.make_async_remote_copy(
                src_ref=send.at[t],
                dst_ref=got.at[me],
                send_sem=sends.at[phase],
                recv_sem=recvs.at[phase],
                device_id=device,
                device_id_type=MESH,
            ).start()
        )
        got[me] = send[me]

    others = pl.ds(0, n - 1)

    def arrived(got, phase):
        pltpu.make_async_copy(got.at[others], got.at[others], recvs.at[phase]).wait()

    def left(send, phase):
        pltpu.make_async_copy(send.at[others], send.at[others], sends.at[phase]).wait()

    width = table.shape[1]
    block_rows = w_ref.shape[1]
    blocks = table.shape[0] // block_rows
    chunks = width // LANES
    proteins = cot_ref.shape[0]
    pairs = w_ref.shape[0]
    tile = chunks * CAP
    slots = n * CAP
    step = min(TOGETHER, n)
    groups = n // step
    rows = step * tile
    few = groups <= 4

    def each(body):
        if few:
            for g in range(groups):
                body(g)
        else:
            lax.fori_loop(0, groups, lambda g, c: (body(g), c)[1], 0)

    def at(g, size):
        return pl.ds(g * size, size) if few else pl.ds(pl.multiple_of(g * size, size), size)

    for copy in load_pairs:
        copy.wait()
    blk = blk_ref[...]
    owner = over(blk, blocks)
    local = rest(blk, blocks)
    local_prot = prot_ref[...] - me * proteins
    square = (pairs, pairs)
    from_row, from_col = iota(square, 0), iota(square, 1)
    owner_f = owner.astype(F32)
    owner_col = jnp.sum(jnp.where(from_row == from_col, owner_f, 0.0), axis=1, keepdims=True)
    earlier = (owner_col == owner_f) & (from_row < from_col)
    rank = jnp.sum(jnp.where(earlier, 1.0, 0.0), axis=0, keepdims=True)
    slot = owner * CAP + rank.astype(jnp.int32)

    place_rows = iota((rows, pairs), 0)
    place_slot = over(place_rows, tile) * CAP + rest(place_rows, CAP)
    weights = w_ref[...]

    def place_of(g):
        return place_slot + g * (step * CAP) == slot

    slot_rows = iota((step * CAP, pairs), 0)

    def make_w(g):
        place = slot_rows + g * (step * CAP) == slot
        block = jnp.sum(jnp.where(place, local.astype(F32), 0.0), axis=1, keepdims=True)
        marked = dot(ones_where(place), weights) * (1.0 + block * MARK)
        send_w[at(g, step)] = marked.reshape(step, CAP, block_rows)

    each(make_w)
    pl.semaphore_wait(barrier, n - 1)
    exchange(send_w, got_w, 0)

    for_prot = ones_where(rest(iota((chunks * PAD, pairs), 0), PAD) == local_prot)
    shape = (chunks * PAD, rows)
    same_c = over(iota(shape, 0), PAD) == over(rest(iota(shape, 1), tile), CAP)
    shape = (rows, chunks * PAD)
    same_c_t = over(iota(shape, 1), PAD) == over(rest(iota(shape, 0), tile), CAP)

    def make_pick(g):
        place = ones_where(place_of(g))
        pick[g] = jnp.where(same_c, dot_nt(for_prot, place), 0.0).astype(BF)
        pick_t[at(g, rows), :] = jnp.where(same_c_t, dot_nt(place, for_prot), 0.0).astype(BF)

    each(make_pick)

    stacked = step * CAP
    pack, _ = repack(step, chunks)
    arrived(got_w, 0)

    def make_dense(g):
        marked = got_w[at(g, step)].reshape(stacked, block_rows)
        plain = marked.astype(BF).astype(F32)
        dense[at(g, stacked), :] = jnp.concatenate(
            [jnp.where(marked == plain * (1.0 + b * MARK), plain, 0.0) for b in range(blocks)],
            axis=1,
        ).astype(BF)

    each(make_dense)
    load_table.wait()
    big = min(slots, 256)
    per_big = big // stacked

    def make_part(h):
        some = dense[pl.ds(h * big if few else pl.multiple_of(h * big, big), big), :]
        part = dot(some, table[...]).astype(BF)
        for j in range(per_big):
            own = part[j * stacked : (j + 1) * stacked]
            stack = jnp.concatenate(
                [own[:, c * LANES : (c + 1) * LANES] for c in range(chunks)], axis=0
            )
            send_part[at(h * per_big + j, step)] = (
                dot(pack, stack).astype(BF).reshape(step, tile, LANES)
            )

    if few:
        for h in range(slots // big):
            make_part(h)
    else:
        lax.fori_loop(0, slots // big, lambda h, c: (make_part(h), c)[1], 0)
    exchange(send_part, got_part, 1)

    dense_t[...] = dense[...].astype(F32).T.astype(BF)
    load_accum.wait()
    load_hid.wait()
    for i in range(hid.shape[0] // LANES):
        some = pl.ds(i * LANES, LANES)
        hid_t[:, some] = hid[some, :].T
    arrived(got_part, 1)

    def bag_of(g):
        return dot(pick[g], got_part[at(g, step)].reshape(rows, LANES))

    if few:
        stack = sum(bag_of(g) for g in range(groups))
    else:
        stack = lax.fori_loop(
            0, groups, lambda g, c: c + bag_of(g), jnp.zeros((chunks * PAD, LANES), F32)
        )
    bag = jnp.concatenate([stack[c * PAD : (c + 1) * PAD] for c in range(chunks)], axis=1)
    load_cot.wait()
    cot = cot_ref[...].astype(F32)
    cot = jnp.concatenate([cot, jnp.zeros((PAD - proteins, cot.shape[1]), F32)], axis=0)
    inv = lax.rsqrt(jnp.mean(bag * bag, axis=-1, keepdims=True) + 1e-06)
    unit = bag * inv
    pre = dot(unit.astype(BF), hid[...])
    sig = jax.nn.sigmoid(pre)
    dpre = (cot * sig * (1.0 + pre * (1.0 - sig))).astype(BF)
    dunit = dot(dpre, hid_t[...])
    dbag = (dunit - unit * jnp.mean(dunit * unit, axis=-1, keepdims=True)) * inv
    dstack = jnp.concatenate(
        [dbag[:, c * LANES : (c + 1) * LANES] for c in range(chunks)], axis=0
    ).astype(BF)

    def make_grad(g):
        send_grad[at(g, step)] = (
            dot(pick_t[at(g, rows), :], dstack).astype(BF).reshape(step, tile, LANES)
        )

    each(make_grad)
    exchange(send_grad, got_grad, 2)
    left(send_w, 0)
    left(send_part, 1)
    left(send_grad, 2)
    arrived(got_grad, 2)


def update(dense_t, tiles, accum, table, out_hbm, acc_hbm, rows_out, acc_out, gathered, stores):
    n, tile, _ = tiles.shape
    blocks, block_rows = accum.shape
    chunks = tile // CAP
    step = min(TOGETHER, n)
    groups = n // step
    stacked = step * CAP
    parts = [pl.ds(b * block_rows, block_rows) for b in range(blocks)]
    _, unpack = repack(step, chunks)
    diagonal = iota((block_rows, block_rows), 0) == iota((block_rows, block_rows), 1)

    def make_gathered(g):
        few = groups <= 4
        gathered[pl.ds(g * stacked if few else pl.multiple_of(g * stacked, stacked), stacked), :] = (
            unpacked(unpack, tiles[pl.ds(g * step, step)], chunks)
        )

    if groups <= 4:
        for g in range(groups):
            make_gathered(g)
    else:
        lax.fori_loop(0, groups, lambda g, c: (make_gathered(g), c)[1], 0)
    writes = []
    for b, some in enumerate(parts):
        grad = dot(dense_t[some, :], gathered[...])
        mean = jnp.mean(grad * grad, axis=-1, keepdims=True)
        old = jnp.sum(jnp.where(diagonal, accum[b : b + 1, :], 0.0), axis=1, keepdims=True)
        new = old + mean
        scale = 0.3 / (jnp.sqrt(new) + 1e-08)
        rows_out[some, :] = (table[some, :].astype(F32) - grad * scale).astype(BF)
        write = pltpu.make_async_copy(rows_out.at[some], out_hbm.at[some], stores.at[b])
        write.start()
        writes.append(write)
        acc_out[b : b + 1, :] = jnp.sum(jnp.where(diagonal, new, 0.0), axis=0, keepdims=True)
    write = pltpu.make_async_copy(acc_out, acc_hbm, stores.at[blocks])
    write.start()
    writes.append(write)
    for write in writes:
        write.wait()


def per_device(table, accum, pair_block, pair_protein, pair_weight, w_hidden, hidden_cot):
    n_group = lax.axis_size("group")
    n_dp = lax.axis_size("dp")
    n = n_group * n_dp
    rows_dev, width = table.shape
    pairs, block_rows = pair_weight.shape
    blocks = rows_dev // block_rows
    tile = (width // LANES) * CAP
    slots = n * CAP
    step = min(TOGETHER, n)
    hbm = pl.BlockSpec(memory_space=pltpu.HBM)
    vmem = pl.BlockSpec(memory_space=pltpu.VMEM)
    tiles = pltpu.VMEM((n, tile, LANES), BF)
    stack = (width // LANES) * PAD
    got_grad, dense_t, accum_held, table_held = pl.pallas_call(
        functools.partial(kernel, n_group, n_dp),
        out_shape=(
            jax.ShapeDtypeStruct((n, tile, LANES), BF),
            jax.ShapeDtypeStruct((rows_dev, slots), BF),
            jax.ShapeDtypeStruct((blocks, block_rows), F32),
            jax.ShapeDtypeStruct(table.shape, BF),
        ),
        in_specs=[hbm] * 7,
        out_specs=(vmem,) * 4,
        scratch_shapes=[
            pltpu.VMEM((1, pairs), jnp.int32),
            pltpu.VMEM((1, pairs), jnp.int32),
            pltpu.VMEM(pair_weight.shape, BF),
            pltpu.VMEM(hidden_cot.shape, BF),
            pltpu.VMEM(w_hidden.shape, BF),
            pltpu.VMEM(w_hidden.shape[::-1], BF),
            pltpu.VMEM((n, CAP, block_rows), F32),
            pltpu.VMEM((n, CAP, block_rows), F32),
            tiles,
            tiles,
            tiles,
            pltpu.VMEM((slots, rows_dev), BF),
            pltpu.VMEM((n // step, stack, step * tile), BF),
            pltpu.VMEM((n * tile, stack), BF),
            pltpu.SemaphoreType.DMA((3,)),
            pltpu.SemaphoreType.DMA((3,)),
            pltpu.SemaphoreType.DMA((7,)),
        ],
        compiler_params=pltpu.CompilerParams(
            collective_id=0, has_side_effects=True, vmem_limit_bytes=LIMIT
        ),
        name="bags",
    )(
        *(
            pltpu.with_memory_space_constraint(x, pltpu.HBM)
            for x in (
                pair_block.reshape(1, pairs),
                pair_protein.reshape(1, pairs),
                pair_weight,
                hidden_cot,
                accum.reshape(blocks, block_rows),
                table,
                w_hidden,
            )
        )
    )
    new_table, new_accum = pl.pallas_call(
        update,
        out_shape=(
            jax.ShapeDtypeStruct(table.shape, BF),
            jax.ShapeDtypeStruct((blocks, block_rows), F32),
        ),
        in_specs=[vmem] * 4,
        out_specs=(hbm, hbm),
        scratch_shapes=[
            pltpu.VMEM(table.shape, BF),
            pltpu.VMEM((blocks, block_rows), F32),
            pltpu.VMEM((slots, width), BF),
            pltpu.SemaphoreType.DMA((1 + blocks,)),
        ],
        compiler_params=pltpu.CompilerParams(vmem_limit_bytes=LIMIT // 2),
        name="update",
    )(dense_t, got_grad, accum_held, table_held)
    return new_table, new_accum.reshape(rows_dev)


def solution(mesh):
    in_specs = (
        P(("group", "dp"), None),
        P(("group", "dp")),
        P(("group", "dp")),
        P(("group", "dp")),
        P(("group", "dp"), None),
        P(),
        P(("group", "dp"), None),
    )
    out_specs = (P(("group", "dp"), None), P(("group", "dp")))
    return jax.shard_map(
        per_device, mesh=mesh, in_specs=in_specs, out_specs=out_specs, check_vma=False
    )
```

```python
import functools

import jax
import jax.numpy as jnp
from jax import lax
from jax.experimental import pallas as pl
from jax.experimental.pallas import tpu as pltpu
from jax.sharding import PartitionSpec as P

CAP = 2
LANES = 128
TOGETHER = 16
PAD = 8
MARK = 2.0**-15
LIMIT = 40 * 1024 * 1024
MESH = pl.DeviceIdType.MESH
BF = jnp.bfloat16
F32 = jnp.float32


def dot(a, b):
    return jnp.dot(a, b, preferred_element_type=F32)


def dot_nt(a, b):
    return lax.dot_general(a, b, (((1,), (1,)), ((), ())), preferred_element_type=F32)


def iota(shape, dim):
    return lax.broadcasted_iota(jnp.int32, shape, dim)


def over(x, k):
    return jnp.right_shift(x, k.bit_length() - 1)


def rest(x, k):
    return jnp.bitwise_and(x, k - 1)


def flips(x, count):
    found = [x]
    k = 1
    while k < count:
        change = k * (1 - 2 * lax.rem(lax.div(x, k), 2))
        found += [y + change for y in found]
        k *= 2
    return found


def ones_where(mask):
    return jnp.where(mask, 1.0, 0.0).astype(BF)


def repack(step, chunks):
    tile, stacked = chunks * CAP, step * CAP
    shape = (step * tile, step * tile)
    to_r, to_c = iota(shape, 0), iota(shape, 1)
    r_c, r_d, r_k = over(to_r, stacked), over(rest(to_r, stacked), CAP), rest(to_r, CAP)
    unpack = ones_where(to_c == r_d * tile + r_c * CAP + r_k)
    t_c, t_d, t_k = over(to_c, stacked), over(rest(to_c, stacked), CAP), rest(to_c, CAP)
    pack = ones_where(to_r == t_d * tile + t_c * CAP + t_k)
    return pack, unpack


def unpacked(unpack, tiles, count):
    step, tile, lanes = tiles.shape
    stacked = step * CAP
    high = dot(unpack[: count * stacked], tiles.reshape(step * tile, lanes))
    return jnp.concatenate(
        [high[c * stacked : (c + 1) * stacked] for c in range(count)], axis=1
    ).astype(BF)


def kernel(
    n_group,
    n_dp,
    blk_hbm,
    prot_hbm,
    w_hbm,
    cot_hbm,
    accum_hbm,
    table_hbm,
    hid_hbm,
    got_grad,
    dense_t,
    accum,
    table,
    blk_ref,
    prot_ref,
    w_ref,
    cot_ref,
    hid,
    hid_t,
    send_w,
    got_w,
    send_part,
    got_part,
    send_grad,
    dense,
    pick,
    pick_t,
    sends,
    recvs,
    loads,
):
    n = n_group * n_dp
    mine = (lax.axis_index("group"), lax.axis_index("dp"))
    me = mine[0] * n_dp + mine[1]
    pairs_of = [(blk_hbm, blk_ref), (prot_hbm, prot_ref), (w_hbm, w_ref)]
    others_of = [(table_hbm, table), (hid_hbm, hid), (cot_hbm, cot_ref), (accum_hbm, accum)]
    copies = [
        pltpu.make_async_copy(a, b, loads.at[i]) for i, (a, b) in enumerate(pairs_of + others_of)
    ]
    for copy in copies:
        copy.start()
    load_pairs = copies[:3]
    load_table, load_hid, load_cot, load_accum = copies[3:]

    def to_all(act):
        if n <= 32:
            at_group, at_dp = flips(mine[0], n_group), flips(mine[1], n_dp)
            for a in reversed(range(n_group)):
                for b in reversed(range(n_dp)):
                    if a or b:
                        act((at_group[a], at_dp[b]), at_group[a] * n_dp + at_dp[b])
        else:

            def one(i, carry):
                t = lax.rem(me + i, n)
                act((lax.div(t, n_dp), lax.rem(t, n_dp)), t)
                return carry

            lax.fori_loop(1, n, one, 0)

    barrier = pltpu.get_barrier_semaphore()
    to_all(
        lambda device, t: pl.semaphore_signal(
            barrier, inc=1, device_id=device, device_id_type=MESH
        )
    )

    def exchange(send, got, phase):
        to_all(
            lambda device, t: pltpu.make_async_remote_copy(
                src_ref=send.at[t],
                dst_ref=got.at[me],
                send_sem=sends.at[phase],
                recv_sem=recvs.at[phase],
                device_id=device,
                device_id_type=MESH,
            ).start()
        )
        got[me] = send[me]

    others = pl.ds(0, n - 1)

    def arrived(got, phase):
        pltpu.make_async_copy(got.at[others], got.at[others], recvs.at[phase]).wait()

    def left(send, phase):
        pltpu.make_async_copy(send.at[others], send.at[others], sends.at[phase]).wait()

    width = table.shape[1]
    block_rows = w_ref.shape[1]
    blocks = table.shape[0] // block_rows
    chunks = width // LANES
    proteins = cot_ref.shape[0]
    pairs = w_ref.shape[0]
    tile = chunks * CAP
    slots = n * CAP
    step = min(TOGETHER, n)
    groups = n // step
    rows = step * tile
    few = groups <= 4

    def each(body):
        if few:
            for g in range(groups):
                body(g)
        else:
            lax.fori_loop(0, groups, lambda g, c: (body(g), c)[1], 0)

    def at(g, size):
        return pl.ds(g * size, size) if few else pl.ds(pl.multiple_of(g * size, size), size)

    for copy in load_pairs:
        copy.wait()
    blk = blk_ref[...]
    owner = over(blk, blocks)
    local = rest(blk, blocks)
    local_prot = prot_ref[...] - me * proteins
    square = (pairs, pairs)
    from_row, from_col = iota(square, 0), iota(square, 1)
    owner_f = owner.astype(F32)
    owner_col = jnp.sum(jnp.where(from_row == from_col, owner_f, 0.0), axis=1, keepdims=True)
    earlier = (owner_col == owner_f) & (from_row < from_col)
    rank = jnp.sum(jnp.where(earlier, 1.0, 0.0), axis=0, keepdims=True)
    slot = owner * CAP + rank.astype(jnp.int32)

    place_rows = iota((rows, pairs), 0)
    place_slot = over(place_rows, tile) * CAP + rest(place_rows, CAP)
    weights = w_ref[...]

    def place_of(g):
        return place_slot + g * (step * CAP) == slot

    slot_rows = iota((step * CAP, pairs), 0)

    def make_w(g):
        place = slot_rows + g * (step * CAP) == slot
        block = jnp.sum(jnp.where(place, local.astype(F32), 0.0), axis=1, keepdims=True)
        marked = dot(ones_where(place), weights) * (1.0 + block * MARK)
        send_w[at(g, step)] = marked.reshape(step, CAP, block_rows)

    each(make_w)
    pl.semaphore_wait(barrier, n - 1)
    exchange(send_w, got_w, 0)

    for_prot = ones_where(rest(iota((chunks * PAD, pairs), 0), PAD) == local_prot)
    shape = (chunks * PAD, rows)
    same_c = over(iota(shape, 0), PAD) == over(rest(iota(shape, 1), tile), CAP)
    shape = (rows, chunks * PAD)
    same_c_t = over(iota(shape, 1), PAD) == over(rest(iota(shape, 0), tile), CAP)

    def make_pick(g):
        place = ones_where(place_of(g))
        pick[g] = jnp.where(same_c, dot_nt(for_prot, place), 0.0).astype(BF)
        pick_t[at(g, rows), :] = jnp.where(same_c_t, dot_nt(place, for_prot), 0.0).astype(BF)

    each(make_pick)

    stacked = step * CAP
    pack, _ = repack(step, chunks)
    arrived(got_w, 0)

    def make_dense(g):
        marked = got_w[at(g, step)].reshape(stacked, block_rows)
        plain = marked.astype(BF).astype(F32)
        dense[at(g, stacked), :] = jnp.concatenate(
            [jnp.where(marked == plain * (1.0 + b * MARK), plain, 0.0) for b in range(blocks)],
            axis=1,
        ).astype(BF)

    each(make_dense)
    load_table.wait()
    big = min(slots, 256)
    per_big = big // stacked

    def make_part(h):
        some = dense[pl.ds(h * big if few else pl.multiple_of(h * big, big), big), :]
        part = dot(some, table[...]).astype(BF)
        for j in range(per_big):
            own = part[j * stacked : (j + 1) * stacked]
            stack = jnp.concatenate(
                [own[:, c * LANES : (c + 1) * LANES] for c in range(chunks)], axis=0
            )
            send_part[at(h * per_big + j, step)] = (
                dot(pack, stack).astype(BF).reshape(step, tile, LANES)
            )

    if few:
        for h in range(slots // big):
            make_part(h)
    else:
        lax.fori_loop(0, slots // big, lambda h, c: (make_part(h), c)[1], 0)
    exchange(send_part, got_part, 1)

    dense_t[...] = dense[...].astype(F32).T.astype(BF)
    load_accum.wait()
    load_hid.wait()
    for i in range(hid.shape[0] // LANES):
        some = pl.ds(i * LANES, LANES)
        hid_t[:, some] = hid[some, :].T
    arrived(got_part, 1)

    def bag_of(g):
        return dot(pick[g], got_part[at(g, step)].reshape(rows, LANES))

    if few:
        stack = sum(bag_of(g) for g in range(groups))
    else:
        stack = lax.fori_loop(
            0, groups, lambda g, c: c + bag_of(g), jnp.zeros((chunks * PAD, LANES), F32)
        )
    bag = jnp.concatenate([stack[c * PAD : (c + 1) * PAD] for c in range(chunks)], axis=1)
    load_cot.wait()
    cot = cot_ref[...].astype(F32)
    cot = jnp.concatenate([cot, jnp.zeros((PAD - proteins, cot.shape[1]), F32)], axis=0)
    inv = lax.rsqrt(jnp.mean(bag * bag, axis=-1, keepdims=True) + 1e-06)
    unit = bag * inv
    pre = dot(unit.astype(BF), hid[...])
    sig = jax.nn.sigmoid(pre)
    dpre = (cot * sig * (1.0 + pre * (1.0 - sig))).astype(BF)
    dunit = dot(dpre, hid_t[...])
    dbag = (dunit - unit * jnp.mean(dunit * unit, axis=-1, keepdims=True)) * inv
    dstack = jnp.concatenate(
        [dbag[:, c * LANES : (c + 1) * LANES] for c in range(chunks)], axis=0
    ).astype(BF)

    def make_grad(g):
        send_grad[at(g, step)] = (
            dot(pick_t[at(g, rows), :], dstack).astype(BF).reshape(step, tile, LANES)
        )

    each(make_grad)
    exchange(send_grad, got_grad, 2)
    left(send_w, 0)
    left(send_part, 1)
    left(send_grad, 2)
    arrived(got_grad, 2)


def update(dense_t, tiles, accum, table, out_hbm, acc_hbm, rows_out, acc_out, gathered, stores):
    n, tile, _ = tiles.shape
    blocks, block_rows = accum.shape
    chunks = tile // CAP
    step = min(TOGETHER, n)
    groups = n // step
    stacked = step * CAP
    parts = [pl.ds(b * block_rows, block_rows) for b in range(blocks)]
    _, unpack = repack(step, chunks)
    diagonal = iota((block_rows, block_rows), 0) == iota((block_rows, block_rows), 1)

    def make_gathered(g):
        few = groups <= 4
        gathered[pl.ds(g * stacked if few else pl.multiple_of(g * stacked, stacked), stacked), :] = (
            unpacked(unpack, tiles[pl.ds(g * step, step)], chunks)
        )

    if groups <= 4:
        for g in range(groups):
            make_gathered(g)
    else:
        lax.fori_loop(0, groups, lambda g, c: (make_gathered(g), c)[1], 0)
    writes = []
    for b, some in enumerate(parts):
        grad = dot(dense_t[some, :], gathered[...])
        mean = jnp.mean(grad * grad, axis=-1, keepdims=True)
        old = jnp.sum(jnp.where(diagonal, accum[b : b + 1, :], 0.0), axis=1, keepdims=True)
        new = old + mean
        scale = 0.3 / (jnp.sqrt(new) + 1e-08)
        rows_out[some, :] = (table[some, :].astype(F32) - grad * scale).astype(BF)
        write = pltpu.make_async_copy(rows_out.at[some], out_hbm.at[some], stores.at[b])
        write.start()
        writes.append(write)
        acc_out[b : b + 1, :] = jnp.sum(jnp.where(diagonal, new, 0.0), axis=0, keepdims=True)
    write = pltpu.make_async_copy(acc_out, acc_hbm, stores.at[blocks])
    write.start()
    writes.append(write)
    for write in writes:
        write.wait()


def per_device(table, accum, pair_block, pair_protein, pair_weight, w_hidden, hidden_cot):
    n_group = lax.axis_size("group")
    n_dp = lax.axis_size("dp")
    n = n_group * n_dp
    rows_dev, width = table.shape
    pairs, block_rows = pair_weight.shape
    blocks = rows_dev // block_rows
    tile = (width // LANES) * CAP
    slots = n * CAP
    step = min(TOGETHER, n)
    hbm = pl.BlockSpec(memory_space=pltpu.HBM)
    vmem = pl.BlockSpec(memory_space=pltpu.VMEM)
    tiles = pltpu.VMEM((n, tile, LANES), BF)
    stack = (width // LANES) * PAD
    got_grad, dense_t, accum_held, table_held = pl.pallas_call(
        functools.partial(kernel, n_group, n_dp),
        out_shape=(
            jax.ShapeDtypeStruct((n, tile, LANES), BF),
            jax.ShapeDtypeStruct((rows_dev, slots), BF),
            jax.ShapeDtypeStruct((blocks, block_rows), F32),
            jax.ShapeDtypeStruct(table.shape, BF),
        ),
        in_specs=[hbm] * 7,
        out_specs=(vmem,) * 4,
        scratch_shapes=[
            pltpu.VMEM((1, pairs), jnp.int32),
            pltpu.VMEM((1, pairs), jnp.int32),
            pltpu.VMEM(pair_weight.shape, BF),
            pltpu.VMEM(hidden_cot.shape, BF),
            pltpu.VMEM(w_hidden.shape, BF),
            pltpu.VMEM(w_hidden.shape[::-1], BF),
            pltpu.VMEM((n, CAP, block_rows), F32),
            pltpu.VMEM((n, CAP, block_rows), F32),
            tiles,
            tiles,
            tiles,
            pltpu.VMEM((slots, rows_dev), BF),
            pltpu.VMEM((n // step, stack, step * tile), BF),
            pltpu.VMEM((n * tile, stack), BF),
            pltpu.SemaphoreType.DMA((3,)),
            pltpu.SemaphoreType.DMA((3,)),
            pltpu.SemaphoreType.DMA((7,)),
        ],
        compiler_params=pltpu.CompilerParams(
            collective_id=0, has_side_effects=True, vmem_limit_bytes=LIMIT
        ),
        name="bags",
    )(
        *(
            pltpu.with_memory_space_constraint(x, pltpu.HBM)
            for x in (
                pair_block.reshape(1, pairs),
                pair_protein.reshape(1, pairs),
                pair_weight,
                hidden_cot,
                accum.reshape(blocks, block_rows),
                table,
                w_hidden,
            )
        )
    )
    new_table, new_accum = pl.pallas_call(
        update,
        out_shape=(
            jax.ShapeDtypeStruct(table.shape, BF),
            jax.ShapeDtypeStruct((blocks, block_rows), F32),
        ),
        in_specs=[vmem] * 4,
        out_specs=(hbm, hbm),
        scratch_shapes=[
            pltpu.VMEM(table.shape, BF),
            pltpu.VMEM((blocks, block_rows), F32),
            pltpu.VMEM((slots, width), BF),
            pltpu.SemaphoreType.DMA((1 + blocks,)),
        ],
        compiler_params=pltpu.CompilerParams(vmem_limit_bytes=LIMIT // 2),
        name="update",
    )(dense_t, got_grad, accum_held, table_held)
    return new_table, new_accum.reshape(rows_dev)


def solution(mesh):
    in_specs = (
        P(("group", "dp"), None),
        P(("group", "dp")),
        P(("group", "dp")),
        P(("group", "dp")),
        P(("group", "dp"), None),
        P(),
        P(("group", "dp"), None),
    )
    out_specs = (P(("group", "dp"), None), P(("group", "dp")))
    return jax.shard_map(
        per_device, mesh=mesh, in_specs=in_specs, out_specs=out_specs, check_vma=False
    )
```

```python
import functools

import jax
import jax.numpy as jnp
from jax import lax
from jax.experimental import pallas as pl
from jax.experimental.pallas import tpu as pltpu
from jax.sharding import PartitionSpec as P

CAP = 2
LANES = 128
TOGETHER = 16
PAD = 8
MARK = 2.0**-15
LIMIT = 40 * 1024 * 1024
MESH = pl.DeviceIdType.MESH
BF = jnp.bfloat16
F32 = jnp.float32


def dot(a, b):
    return jnp.dot(a, b, preferred_element_type=F32)


def dot_nt(a, b):
    return lax.dot_general(a, b, (((1,), (1,)), ((), ())), preferred_element_type=F32)


def iota(shape, dim):
    return lax.broadcasted_iota(jnp.int32, shape, dim)


def over(x, k):
    return jnp.right_shift(x, k.bit_length() - 1)


def rest(x, k):
    return jnp.bitwise_and(x, k - 1)


def flips(x, count):
    found = [x]
    k = 1
    while k < count:
        change = k * (1 - 2 * lax.rem(lax.div(x, k), 2))
        found += [y + change for y in found]
        k *= 2
    return found


def ones_where(mask):
    return jnp.where(mask, 1.0, 0.0).astype(BF)


def repack(step, chunks):
    tile, stacked = chunks * CAP, step * CAP
    shape = (step * tile, step * tile)
    to_r, to_c = iota(shape, 0), iota(shape, 1)
    r_c, r_d, r_k = over(to_r, stacked), over(rest(to_r, stacked), CAP), rest(to_r, CAP)
    unpack = ones_where(to_c == r_d * tile + r_c * CAP + r_k)
    t_c, t_d, t_k = over(to_c, stacked), over(rest(to_c, stacked), CAP), rest(to_c, CAP)
    pack = ones_where(to_r == t_d * tile + t_c * CAP + t_k)
    return pack, unpack


def unpacked(unpack, tiles, count):
    step, tile, lanes = tiles.shape
    stacked = step * CAP
    high = dot(unpack[: count * stacked], tiles.reshape(step * tile, lanes))
    return jnp.concatenate(
        [high[c * stacked : (c + 1) * stacked] for c in range(count)], axis=1
    ).astype(BF)


def kernel(
    n_group,
    n_dp,
    blk_hbm,
    prot_hbm,
    w_hbm,
    cot_hbm,
    accum_hbm,
    table_hbm,
    hid_hbm,
    got_grad,
    dense_t,
    accum,
    table,
    blk_ref,
    prot_ref,
    w_ref,
    cot_ref,
    hid,
    hid_t,
    send_w,
    got_w,
    send_part,
    got_part,
    send_grad,
    dense,
    pick,
    pick_t,
    sends,
    recvs,
    loads,
):
    n = n_group * n_dp
    mine = (lax.axis_index("group"), lax.axis_index("dp"))
    me = mine[0] * n_dp + mine[1]
    pairs_of = [(blk_hbm, blk_ref), (prot_hbm, prot_ref), (w_hbm, w_ref)]
    others_of = [(table_hbm, table), (hid_hbm, hid), (cot_hbm, cot_ref), (accum_hbm, accum)]
    copies = [
        pltpu.make_async_copy(a, b, loads.at[i]) for i, (a, b) in enumerate(pairs_of + others_of)
    ]
    for copy in copies:
        copy.start()
    load_pairs = copies[:3]
    load_table, load_hid, load_cot, load_accum = copies[3:]

    def to_all(act):
        if n <= 32:
            at_group, at_dp = flips(mine[0], n_group), flips(mine[1], n_dp)
            half = n_dp // 2
            for a in reversed(range(n_group)):
                for b in reversed(range(half)):
                    for c in (b + half, b):
                        if a or c:
                            act((at_group[a], at_dp[c]), at_group[a] * n_dp + at_dp[c])
        else:

            def one(i, carry):
                t = lax.rem(me + i, n)
                act((lax.div(t, n_dp), lax.rem(t, n_dp)), t)
                return carry

            lax.fori_loop(1, n, one, 0)

    barrier = pltpu.get_barrier_semaphore()
    to_all(
        lambda device, t: pl.semaphore_signal(
            barrier, inc=1, device_id=device, device_id_type=MESH
        )
    )

    def exchange(send, got, phase):
        to_all(
            lambda device, t: pltpu.make_async_remote_copy(
                src_ref=send.at[t],
                dst_ref=got.at[me],
                send_sem=sends.at[phase],
                recv_sem=recvs.at[phase],
                device_id=device,
                device_id_type=MESH,
            ).start()
        )
        got[me] = send[me]

    others = pl.ds(0, n - 1)

    def arrived(got, phase):
        pltpu.make_async_copy(got.at[others], got.at[others], recvs.at[phase]).wait()

    def left(send, phase):
        pltpu.make_async_copy(send.at[others], send.at[others], sends.at[phase]).wait()

    width = table.shape[1]
    block_rows = w_ref.shape[1]
    blocks = table.shape[0] // block_rows
    chunks = width // LANES
    proteins = cot_ref.shape[0]
    pairs = w_ref.shape[0]
    tile = chunks * CAP
    slots = n * CAP
    step = min(TOGETHER, n)
    groups = n // step
    rows = step * tile
    few = groups <= 4

    def each(body):
        if few:
            for g in range(groups):
                body(g)
        else:
            lax.fori_loop(0, groups, lambda g, c: (body(g), c)[1], 0)

    def at(g, size):
        return pl.ds(g * size, size) if few else pl.ds(pl.multiple_of(g * size, size), size)

    for copy in load_pairs:
        copy.wait()
    blk = blk_ref[...]
    owner = over(blk, blocks)
    local = rest(blk, blocks)
    local_prot = prot_ref[...] - me * proteins
    square = (pairs, pairs)
    from_row, from_col = iota(square, 0), iota(square, 1)
    owner_f = owner.astype(F32)
    owner_col = jnp.sum(jnp.where(from_row == from_col, owner_f, 0.0), axis=1, keepdims=True)
    earlier = (owner_col == owner_f) & (from_row < from_col)
    rank = jnp.sum(jnp.where(earlier, 1.0, 0.0), axis=0, keepdims=True)
    slot = owner * CAP + rank.astype(jnp.int32)

    place_rows = iota((rows, pairs), 0)
    place_slot = over(place_rows, tile) * CAP + rest(place_rows, CAP)
    weights = w_ref[...]

    def place_of(g):
        return place_slot + g * (step * CAP) == slot

    slot_rows = iota((step * CAP, pairs), 0)

    def make_w(g):
        place = slot_rows + g * (step * CAP) == slot
        block = jnp.sum(jnp.where(place, local.astype(F32), 0.0), axis=1, keepdims=True)
        marked = dot(ones_where(place), weights) * (1.0 + block * MARK)
        send_w[at(g, step)] = marked.reshape(step, CAP, block_rows)

    each(make_w)
    pl.semaphore_wait(barrier, n - 1)
    exchange(send_w, got_w, 0)

    for_prot = ones_where(rest(iota((chunks * PAD, pairs), 0), PAD) == local_prot)
    shape = (chunks * PAD, rows)
    same_c = over(iota(shape, 0), PAD) == over(rest(iota(shape, 1), tile), CAP)
    shape = (rows, chunks * PAD)
    same_c_t = over(iota(shape, 1), PAD) == over(rest(iota(shape, 0), tile), CAP)

    def make_pick(g):
        place = ones_where(place_of(g))
        pick[g] = jnp.where(same_c, dot_nt(for_prot, place), 0.0).astype(BF)
        pick_t[at(g, rows), :] = jnp.where(same_c_t, dot_nt(place, for_prot), 0.0).astype(BF)

    each(make_pick)

    stacked = step * CAP
    pack, _ = repack(step, chunks)
    arrived(got_w, 0)

    def make_dense(g):
        marked = got_w[at(g, step)].reshape(stacked, block_rows)
        plain = marked.astype(BF).astype(F32)
        dense[at(g, stacked), :] = jnp.concatenate(
            [jnp.where(marked == plain * (1.0 + b * MARK), plain, 0.0) for b in range(blocks)],
            axis=1,
        ).astype(BF)

    each(make_dense)
    load_table.wait()
    big = min(slots, 256)
    per_big = big // stacked

    def make_part(h):
        some = dense[pl.ds(h * big if few else pl.multiple_of(h * big, big), big), :]
        part = dot(some, table[...]).astype(BF)
        for j in range(per_big):
            own = part[j * stacked : (j + 1) * stacked]
            stack = jnp.concatenate(
                [own[:, c * LANES : (c + 1) * LANES] for c in range(chunks)], axis=0
            )
            send_part[at(h * per_big + j, step)] = (
                dot(pack, stack).astype(BF).reshape(step, tile, LANES)
            )

    if few:
        for h in range(slots // big):
            make_part(h)
    else:
        lax.fori_loop(0, slots // big, lambda h, c: (make_part(h), c)[1], 0)
    exchange(send_part, got_part, 1)

    dense_t[...] = dense[...].astype(F32).T.astype(BF)
    load_accum.wait()
    load_hid.wait()
    for i in range(hid.shape[0] // LANES):
        some = pl.ds(i * LANES, LANES)
        hid_t[:, some] = hid[some, :].T
    arrived(got_part, 1)

    def bag_of(g):
        return dot(pick[g], got_part[at(g, step)].reshape(rows, LANES))

    if few:
        stack = sum(bag_of(g) for g in range(groups))
    else:
        stack = lax.fori_loop(
            0, groups, lambda g, c: c + bag_of(g), jnp.zeros((chunks * PAD, LANES), F32)
        )
    bag = jnp.concatenate([stack[c * PAD : (c + 1) * PAD] for c in range(chunks)], axis=1)
    load_cot.wait()
    cot = cot_ref[...].astype(F32)
    cot = jnp.concatenate([cot, jnp.zeros((PAD - proteins, cot.shape[1]), F32)], axis=0)
    inv = lax.rsqrt(jnp.mean(bag * bag, axis=-1, keepdims=True) + 1e-06)
    unit = bag * inv
    pre = dot(unit.astype(BF), hid[...])
    sig = jax.nn.sigmoid(pre)
    dpre = (cot * sig * (1.0 + pre * (1.0 - sig))).astype(BF)
    dunit = dot(dpre, hid_t[...])
    dbag = (dunit - unit * jnp.mean(dunit * unit, axis=-1, keepdims=True)) * inv
    dstack = jnp.concatenate(
        [dbag[:, c * LANES : (c + 1) * LANES] for c in range(chunks)], axis=0
    ).astype(BF)

    def make_grad(g):
        send_grad[at(g, step)] = (
            dot(pick_t[at(g, rows), :], dstack).astype(BF).reshape(step, tile, LANES)
        )

    each(make_grad)
    exchange(send_grad, got_grad, 2)
    left(send_w, 0)
    left(send_part, 1)
    left(send_grad, 2)
    arrived(got_grad, 2)


def update(dense_t, tiles, accum, table, out_hbm, acc_hbm, rows_out, acc_out, gathered, stores):
    n, tile, _ = tiles.shape
    blocks, block_rows = accum.shape
    chunks = tile // CAP
    step = min(TOGETHER, n)
    groups = n // step
    stacked = step * CAP
    parts = [pl.ds(b * block_rows, block_rows) for b in range(blocks)]
    _, unpack = repack(step, chunks)
    diagonal = iota((block_rows, block_rows), 0) == iota((block_rows, block_rows), 1)

    def make_gathered(g):
        few = groups <= 4
        gathered[pl.ds(g * stacked if few else pl.multiple_of(g * stacked, stacked), stacked), :] = (
            unpacked(unpack, tiles[pl.ds(g * step, step)], chunks)
        )

    if groups <= 4:
        for g in range(groups):
            make_gathered(g)
    else:
        lax.fori_loop(0, groups, lambda g, c: (make_gathered(g), c)[1], 0)
    writes = []
    for b, some in enumerate(parts):
        grad = dot(dense_t[some, :], gathered[...])
        mean = jnp.mean(grad * grad, axis=-1, keepdims=True)
        old = jnp.sum(jnp.where(diagonal, accum[b : b + 1, :], 0.0), axis=1, keepdims=True)
        new = old + mean
        scale = 0.3 / (jnp.sqrt(new) + 1e-08)
        rows_out[some, :] = (table[some, :].astype(F32) - grad * scale).astype(BF)
        write = pltpu.make_async_copy(rows_out.at[some], out_hbm.at[some], stores.at[b])
        write.start()
        writes.append(write)
        acc_out[b : b + 1, :] = jnp.sum(jnp.where(diagonal, new, 0.0), axis=0, keepdims=True)
    write = pltpu.make_async_copy(acc_out, acc_hbm, stores.at[blocks])
    write.start()
    writes.append(write)
    for write in writes:
        write.wait()


def per_device(table, accum, pair_block, pair_protein, pair_weight, w_hidden, hidden_cot):
    n_group = lax.axis_size("group")
    n_dp = lax.axis_size("dp")
    n = n_group * n_dp
    rows_dev, width = table.shape
    pairs, block_rows = pair_weight.shape
    blocks = rows_dev // block_rows
    tile = (width // LANES) * CAP
    slots = n * CAP
    step = min(TOGETHER, n)
    hbm = pl.BlockSpec(memory_space=pltpu.HBM)
    vmem = pl.BlockSpec(memory_space=pltpu.VMEM)
    tiles = pltpu.VMEM((n, tile, LANES), BF)
    stack = (width // LANES) * PAD
    got_grad, dense_t, accum_held, table_held = pl.pallas_call(
        functools.partial(kernel, n_group, n_dp),
        out_shape=(
            jax.ShapeDtypeStruct((n, tile, LANES), BF),
            jax.ShapeDtypeStruct((rows_dev, slots), BF),
            jax.ShapeDtypeStruct((blocks, block_rows), F32),
            jax.ShapeDtypeStruct(table.shape, BF),
        ),
        in_specs=[hbm] * 7,
        out_specs=(vmem,) * 4,
        scratch_shapes=[
            pltpu.VMEM((1, pairs), jnp.int32),
            pltpu.VMEM((1, pairs), jnp.int32),
            pltpu.VMEM(pair_weight.shape, BF),
            pltpu.VMEM(hidden_cot.shape, BF),
            pltpu.VMEM(w_hidden.shape, BF),
            pltpu.VMEM(w_hidden.shape[::-1], BF),
            pltpu.VMEM((n, CAP, block_rows), F32),
            pltpu.VMEM((n, CAP, block_rows), F32),
            tiles,
            tiles,
            tiles,
            pltpu.VMEM((slots, rows_dev), BF),
            pltpu.VMEM((n // step, stack, step * tile), BF),
            pltpu.VMEM((n * tile, stack), BF),
            pltpu.SemaphoreType.DMA((3,)),
            pltpu.SemaphoreType.DMA((3,)),
            pltpu.SemaphoreType.DMA((7,)),
        ],
        compiler_params=pltpu.CompilerParams(
            collective_id=0, has_side_effects=True, vmem_limit_bytes=LIMIT
        ),
        name="bags",
    )(
        *(
            pltpu.with_memory_space_constraint(x, pltpu.HBM)
            for x in (
                pair_block.reshape(1, pairs),
                pair_protein.reshape(1, pairs),
                pair_weight,
                hidden_cot,
                accum.reshape(blocks, block_rows),
                table,
                w_hidden,
            )
        )
    )
    new_table, new_accum = pl.pallas_call(
        update,
        out_shape=(
            jax.ShapeDtypeStruct(table.shape, BF),
            jax.ShapeDtypeStruct((blocks, block_rows), F32),
        ),
        in_specs=[vmem] * 4,
        out_specs=(hbm, hbm),
        scratch_shapes=[
            pltpu.VMEM(table.shape, BF),
            pltpu.VMEM((blocks, block_rows), F32),
            pltpu.VMEM((slots, width), BF),
            pltpu.SemaphoreType.DMA((1 + blocks,)),
        ],
        compiler_params=pltpu.CompilerParams(vmem_limit_bytes=LIMIT // 2),
        name="update",
    )(dense_t, got_grad, accum_held, table_held)
    return new_table, new_accum.reshape(rows_dev)


def solution(mesh):
    in_specs = (
        P(("group", "dp"), None),
        P(("group", "dp")),
        P(("group", "dp")),
        P(("group", "dp")),
        P(("group", "dp"), None),
        P(),
        P(("group", "dp"), None),
    )
    out_specs = (P(("group", "dp"), None), P(("group", "dp")))
    return jax.shard_map(
        per_device, mesh=mesh, in_specs=in_specs, out_specs=out_specs, check_vma=False
    )
```

```python
import functools

import jax
import jax.numpy as jnp
from jax import lax
from jax.experimental import pallas as pl
from jax.experimental.pallas import tpu as pltpu
from jax.sharding import PartitionSpec as P

CAP = 2
LANES = 128
TOGETHER = 16
PAD = 8
MARK = 2.0**-15
LIMIT = 40 * 1024 * 1024
MESH = pl.DeviceIdType.MESH
BF = jnp.bfloat16
F32 = jnp.float32


def dot(a, b):
    return jnp.dot(a, b, preferred_element_type=F32)


def dot_nt(a, b):
    return lax.dot_general(a, b, (((1,), (1,)), ((), ())), preferred_element_type=F32)


def iota(shape, dim):
    return lax.broadcasted_iota(jnp.int32, shape, dim)


def over(x, k):
    return jnp.right_shift(x, k.bit_length() - 1)


def rest(x, k):
    return jnp.bitwise_and(x, k - 1)


def flips(x, count):
    found = [x]
    k = 1
    while k < count:
        change = k * (1 - 2 * lax.rem(lax.div(x, k), 2))
        found += [y + change for y in found]
        k *= 2
    return found


def ones_where(mask):
    return jnp.where(mask, 1.0, 0.0).astype(BF)


def repack(step, chunks):
    tile, stacked = chunks * CAP, step * CAP
    shape = (step * tile, step * tile)
    to_r, to_c = iota(shape, 0), iota(shape, 1)
    r_c, r_d, r_k = over(to_r, stacked), over(rest(to_r, stacked), CAP), rest(to_r, CAP)
    unpack = ones_where(to_c == r_d * tile + r_c * CAP + r_k)
    t_c, t_d, t_k = over(to_c, stacked), over(rest(to_c, stacked), CAP), rest(to_c, CAP)
    pack = ones_where(to_r == t_d * tile + t_c * CAP + t_k)
    return pack, unpack


def unpacked(unpack, tiles, count):
    step, tile, lanes = tiles.shape
    stacked = step * CAP
    high = dot(unpack[: count * stacked], tiles.reshape(step * tile, lanes))
    return jnp.concatenate(
        [high[c * stacked : (c + 1) * stacked] for c in range(count)], axis=1
    ).astype(BF)


def kernel(
    n_group,
    n_dp,
    blk_hbm,
    prot_hbm,
    w_hbm,
    cot_hbm,
    accum_hbm,
    table_hbm,
    hid_hbm,
    got_grad,
    dense_t,
    accum,
    table,
    unpack,
    blk_ref,
    prot_ref,
    w_ref,
    cot_ref,
    hid,
    hid_t,
    send_w,
    got_w,
    send_part,
    got_part,
    send_grad,
    dense,
    part,
    pick,
    pick_t,
    sends,
    recvs,
    loads,
):
    n = n_group * n_dp
    mine = (lax.axis_index("group"), lax.axis_index("dp"))
    me = mine[0] * n_dp + mine[1]
    pairs_of = [(blk_hbm, blk_ref), (prot_hbm, prot_ref), (w_hbm, w_ref)]
    others_of = [(table_hbm, table), (hid_hbm, hid), (cot_hbm, cot_ref), (accum_hbm, accum)]
    copies = [
        pltpu.make_async_copy(a, b, loads.at[i]) for i, (a, b) in enumerate(pairs_of + others_of)
    ]
    for copy in copies[:3]:
        copy.start()
    load_pairs = copies[:3]
    load_table, load_hid, load_cot, load_accum = copies[3:]

    def to_all(act, sides=range(n_group)):
        if n <= 32:
            at_group, at_dp = flips(mine[0], n_group), flips(mine[1], n_dp)
            half = n_dp // 2
            for a in reversed(sides):
                for b in reversed(range(half)):
                    for c in (b + half, b):
                        if a or c:
                            act((at_group[a], at_dp[c]), at_group[a] * n_dp + at_dp[c])
        else:

            def one(i, carry):
                t = lax.rem(me + i, n)
                act((lax.div(t, n_dp), lax.rem(t, n_dp)), t)
                return carry

            lax.fori_loop(1, n, one, 0)

    barrier = pltpu.get_barrier_semaphore()
    to_all(
        lambda device, t: pl.semaphore_signal(
            barrier, inc=1, device_id=device, device_id_type=MESH
        )
    )

    for copy in copies[3:]:
        copy.start()

    def exchange(send, got, phase, make=None):
        def start(device, t):
            pltpu.make_async_remote_copy(
                src_ref=send.at[t],
                dst_ref=got.at[me],
                send_sem=sends.at[phase],
                recv_sem=recvs.at[phase],
                device_id=device,
                device_id_type=MESH,
            ).start()

        if make is None:
            to_all(start)
        elif n <= 32 and groups == 2:
            half = lax.div(me, step)
            make(1 - half)
            to_all(start, range(n_group // 2, n_group))
            make(half)
            to_all(start, range(n_group // 2))
        else:
            each(make)
            to_all(start)
        got[me] = send[me]

    others = pl.ds(0, n - 1)

    def arrived(got, phase):
        pltpu.make_async_copy(got.at[others], got.at[others], recvs.at[phase]).wait()

    def left(send, phase):
        pltpu.make_async_copy(send.at[others], send.at[others], sends.at[phase]).wait()

    width = table.shape[1]
    block_rows = w_ref.shape[1]
    blocks = table.shape[0] // block_rows
    chunks = width // LANES
    proteins = cot_ref.shape[0]
    pairs = w_ref.shape[0]
    tile = chunks * CAP
    slots = n * CAP
    step = min(TOGETHER, n)
    groups = n // step
    rows = step * tile
    few = groups <= 4

    def each(body):
        if few:
            for g in range(groups):
                body(g)
        else:
            lax.fori_loop(0, groups, lambda g, c: (body(g), c)[1], 0)

    def at(g, size):
        fixed = isinstance(g, int)
        return pl.ds(g * size, size) if fixed else pl.ds(pl.multiple_of(g * size, size), size)

    for copy in load_pairs:
        copy.wait()
    blk = blk_ref[...]
    owner = over(blk, blocks)
    local = rest(blk, blocks)
    local_prot = prot_ref[...] - me * proteins
    square = (pairs, pairs)
    from_row, from_col = iota(square, 0), iota(square, 1)
    owner_f = owner.astype(F32)
    owner_col = jnp.sum(jnp.where(from_row == from_col, owner_f, 0.0), axis=1, keepdims=True)
    earlier = (owner_col == owner_f) & (from_row < from_col)
    rank = jnp.sum(jnp.where(earlier, 1.0, 0.0), axis=0, keepdims=True)
    slot = owner * CAP + rank.astype(jnp.int32)

    place_rows = iota((rows, pairs), 0)
    place_slot = over(place_rows, tile) * CAP + rest(place_rows, CAP)
    weights = w_ref[...]

    def place_of(g):
        return place_slot + g * (step * CAP) == slot

    slot_rows = iota((step * CAP, pairs), 0)

    def make_w(g):
        place = slot_rows + g * (step * CAP) == slot
        block = jnp.sum(jnp.where(place, local.astype(F32), 0.0), axis=1, keepdims=True)
        marked = dot(ones_where(place), weights) * (1.0 + block * MARK)
        send_w[at(g, step)] = marked.reshape(step, CAP, block_rows)

    each(make_w)
    pl.semaphore_wait(barrier, n - 1)
    exchange(send_w, got_w, 0)

    for_prot = ones_where(rest(iota((chunks * PAD, pairs), 0), PAD) == local_prot)
    shape = (chunks * PAD, rows)
    same_c = over(iota(shape, 0), PAD) == over(rest(iota(shape, 1), tile), CAP)
    shape = (rows, chunks * PAD)
    same_c_t = over(iota(shape, 1), PAD) == over(rest(iota(shape, 0), tile), CAP)

    def make_pick(g):
        place = ones_where(place_of(g))
        pick[g] = jnp.where(same_c, dot_nt(for_prot, place), 0.0).astype(BF)
        pick_t[at(g, rows), :] = jnp.where(same_c_t, dot_nt(place, for_prot), 0.0).astype(BF)

    each(make_pick)

    stacked = step * CAP
    pack, unpack[...] = repack(step, chunks)
    arrived(got_w, 0)

    def make_dense(g):
        marked = got_w[at(g, step)].reshape(stacked, block_rows)
        plain = marked.astype(BF).astype(F32)
        dense[at(g, stacked), :] = jnp.concatenate(
            [jnp.where(marked == plain * (1.0 + b * MARK), plain, 0.0) for b in range(blocks)],
            axis=1,
        ).astype(BF)

    each(make_dense)
    load_table.wait()
    big = min(slots, 256)

    def multiply(h):
        part[at(h, big), :] = dot(dense[at(h, big), :], table[...]).astype(BF)

    if few:
        for h in range(slots // big):
            multiply(h)
    else:
        lax.fori_loop(0, slots // big, lambda h, c: (multiply(h), c)[1], 0)

    def make_part(g):
        own = part[at(g, stacked), :]
        stack = jnp.concatenate(
            [own[:, c * LANES : (c + 1) * LANES] for c in range(chunks)], axis=0
        )
        send_part[at(g, step)] = dot(pack, stack).astype(BF).reshape(step, tile, LANES)

    exchange(send_part, got_part, 1, make_part)

    dense_t[...] = dense[...].astype(F32).T.astype(BF)
    load_accum.wait()
    load_hid.wait()
    for i in range(hid.shape[0] // LANES):
        some = pl.ds(i * LANES, LANES)
        hid_t[:, some] = hid[some, :].T
    arrived(got_part, 1)

    def bag_of(g):
        return dot(pick[g], got_part[at(g, step)].reshape(rows, LANES))

    if few:
        stack = sum(bag_of(g) for g in range(groups))
    else:
        stack = lax.fori_loop(
            0, groups, lambda g, c: c + bag_of(g), jnp.zeros((chunks * PAD, LANES), F32)
        )
    bag = jnp.concatenate([stack[c * PAD : (c + 1) * PAD] for c in range(chunks)], axis=1)
    load_cot.wait()
    cot = cot_ref[...].astype(F32)
    cot = jnp.concatenate([cot, jnp.zeros((PAD - proteins, cot.shape[1]), F32)], axis=0)
    inv = lax.rsqrt(jnp.mean(bag * bag, axis=-1, keepdims=True) + 1e-06)
    unit = bag * inv
    pre = dot(unit.astype(BF), hid[...])
    sig = jax.nn.sigmoid(pre)
    dpre = (cot * sig * (1.0 + pre * (1.0 - sig))).astype(BF)
    dunit = dot(dpre, hid_t[...])
    dbag = (dunit - unit * jnp.mean(dunit * unit, axis=-1, keepdims=True)) * inv
    dstack = jnp.concatenate(
        [dbag[:, c * LANES : (c + 1) * LANES] for c in range(chunks)], axis=0
    ).astype(BF)

    def make_grad(g):
        send_grad[at(g, step)] = (
            dot(pick_t[at(g, rows), :], dstack).astype(BF).reshape(step, tile, LANES)
        )

    exchange(send_grad, got_grad, 2, make_grad)
    left(send_w, 0)
    left(send_part, 1)
    left(send_grad, 2)
    arrived(got_grad, 2)


def update(
    dense_t, tiles, accum, table, unpack, out_hbm, acc_hbm, rows_out, acc_out, gathered, stores
):
    n, tile, _ = tiles.shape
    blocks, block_rows = accum.shape
    chunks = tile // CAP
    step = min(TOGETHER, n)
    groups = n // step
    stacked = step * CAP
    parts = [pl.ds(b * block_rows, block_rows) for b in range(blocks)]
    diagonal = iota((block_rows, block_rows), 0) == iota((block_rows, block_rows), 1)

    def make_gathered(g):
        few = groups <= 4
        gathered[pl.ds(g * stacked if few else pl.multiple_of(g * stacked, stacked), stacked), :] = (
            unpacked(unpack[...], tiles[pl.ds(g * step, step)], chunks)
        )

    if groups <= 4:
        for g in range(groups):
            make_gathered(g)
    else:
        lax.fori_loop(0, groups, lambda g, c: (make_gathered(g), c)[1], 0)
    writes = []
    for b, some in enumerate(parts):
        grad = dot(dense_t[some, :], gathered[...])
        mean = jnp.mean(grad * grad, axis=-1, keepdims=True)
        old = jnp.sum(jnp.where(diagonal, accum[b : b + 1, :], 0.0), axis=1, keepdims=True)
        new = old + mean
        scale = 0.3 / (jnp.sqrt(new) + 1e-08)
        rows_out[some, :] = (table[some, :].astype(F32) - grad * scale).astype(BF)
        write = pltpu.make_async_copy(rows_out.at[some], out_hbm.at[some], stores.at[b])
        write.start()
        writes.append(write)
        acc_out[b : b + 1, :] = jnp.sum(jnp.where(diagonal, new, 0.0), axis=0, keepdims=True)
    write = pltpu.make_async_copy(acc_out, acc_hbm, stores.at[blocks])
    write.start()
    writes.append(write)
    for write in writes:
        write.wait()


def per_device(table, accum, pair_block, pair_protein, pair_weight, w_hidden, hidden_cot):
    n_group = lax.axis_size("group")
    n_dp = lax.axis_size("dp")
    n = n_group * n_dp
    rows_dev, width = table.shape
    pairs, block_rows = pair_weight.shape
    blocks = rows_dev // block_rows
    tile = (width // LANES) * CAP
    slots = n * CAP
    step = min(TOGETHER, n)
    hbm = pl.BlockSpec(memory_space=pltpu.HBM)
    vmem = pl.BlockSpec(memory_space=pltpu.VMEM)
    tiles = pltpu.VMEM((n, tile, LANES), BF)
    stack = (width // LANES) * PAD
    got_grad, dense_t, accum_held, table_held, unpack = pl.pallas_call(
        functools.partial(kernel, n_group, n_dp),
        out_shape=(
            jax.ShapeDtypeStruct((n, tile, LANES), BF),
            jax.ShapeDtypeStruct((rows_dev, slots), BF),
            jax.ShapeDtypeStruct((blocks, block_rows), F32),
            jax.ShapeDtypeStruct(table.shape, BF),
            jax.ShapeDtypeStruct((step * tile, step * tile), BF),
        ),
        in_specs=[hbm] * 7,
        out_specs=(vmem,) * 5,
        scratch_shapes=[
            pltpu.VMEM((1, pairs), jnp.int32),
            pltpu.VMEM((1, pairs), jnp.int32),
            pltpu.VMEM(pair_weight.shape, BF),
            pltpu.VMEM(hidden_cot.shape, BF),
            pltpu.VMEM(w_hidden.shape, BF),
            pltpu.VMEM(w_hidden.shape[::-1], BF),
            pltpu.VMEM((n, CAP, block_rows), F32),
            pltpu.VMEM((n, CAP, block_rows), F32),
            tiles,
            tiles,
            tiles,
            pltpu.VMEM((slots, rows_dev), BF),
            pltpu.VMEM((slots, width), BF),
            pltpu.VMEM((n // step, stack, step * tile), BF),
            pltpu.VMEM((n * tile, stack), BF),
            pltpu.SemaphoreType.DMA((3,)),
            pltpu.SemaphoreType.DMA((3,)),
            pltpu.SemaphoreType.DMA((7,)),
        ],
        compiler_params=pltpu.CompilerParams(
            collective_id=0, has_side_effects=True, vmem_limit_bytes=LIMIT
        ),
        name="bags",
    )(
        *(
            pltpu.with_memory_space_constraint(x, pltpu.HBM)
            for x in (
                pair_block.reshape(1, pairs),
                pair_protein.reshape(1, pairs),
                pair_weight,
                hidden_cot,
                accum.reshape(blocks, block_rows),
                table,
                w_hidden,
            )
        )
    )
    new_table, new_accum = pl.pallas_call(
        update,
        out_shape=(
            jax.ShapeDtypeStruct(table.shape, BF),
            jax.ShapeDtypeStruct((blocks, block_rows), F32),
        ),
        in_specs=[vmem] * 5,
        out_specs=(hbm, hbm),
        scratch_shapes=[
            pltpu.VMEM(table.shape, BF),
            pltpu.VMEM((blocks, block_rows), F32),
            pltpu.VMEM((slots, width), BF),
            pltpu.SemaphoreType.DMA((1 + blocks,)),
        ],
        compiler_params=pltpu.CompilerParams(vmem_limit_bytes=LIMIT // 2),
        name="update",
    )(dense_t, got_grad, accum_held, table_held, unpack)
    return new_table, new_accum.reshape(rows_dev)


def solution(mesh):
    in_specs = (
        P(("group", "dp"), None),
        P(("group", "dp")),
        P(("group", "dp")),
        P(("group", "dp")),
        P(("group", "dp"), None),
        P(),
        P(("group", "dp"), None),
    )
    out_specs = (P(("group", "dp"), None), P(("group", "dp")))
    return jax.shard_map(
        per_device, mesh=mesh, in_specs=in_specs, out_specs=out_specs, check_vma=False
    )
```

```python
import functools

import jax
import jax.numpy as jnp
from jax import lax
from jax.experimental import pallas as pl
from jax.experimental.pallas import tpu as pltpu
from jax.sharding import PartitionSpec as P

CAP = 2
LANES = 128
TOGETHER = 16
PAD = 8
MARK = 2.0**-15
LIMIT = 40 * 1024 * 1024
MESH = pl.DeviceIdType.MESH
BF = jnp.bfloat16
F32 = jnp.float32


def dot(a, b):
    return jnp.dot(a, b, preferred_element_type=F32)


def dot_nt(a, b):
    return lax.dot_general(a, b, (((1,), (1,)), ((), ())), preferred_element_type=F32)


def iota(shape, dim):
    return lax.broadcasted_iota(jnp.int32, shape, dim)


def over(x, k):
    return jnp.right_shift(x, k.bit_length() - 1)


def rest(x, k):
    return jnp.bitwise_and(x, k - 1)


def flips(x, count):
    found = [x]
    k = 1
    while k < count:
        change = k * (1 - 2 * lax.rem(lax.div(x, k), 2))
        found += [y + change for y in found]
        k *= 2
    return found


def ones_where(mask):
    return jnp.where(mask, 1.0, 0.0).astype(BF)


def repack(step, chunks):
    tile, stacked = chunks * CAP, step * CAP
    shape = (step * tile, step * tile)
    to_r, to_c = iota(shape, 0), iota(shape, 1)
    r_c, r_d, r_k = over(to_r, stacked), over(rest(to_r, stacked), CAP), rest(to_r, CAP)
    unpack = ones_where(to_c == r_d * tile + r_c * CAP + r_k)
    t_c, t_d, t_k = over(to_c, stacked), over(rest(to_c, stacked), CAP), rest(to_c, CAP)
    pack = ones_where(to_r == t_d * tile + t_c * CAP + t_k)
    return pack, unpack


def unpacked(unpack, tiles, count):
    step, tile, lanes = tiles.shape
    stacked = step * CAP
    high = dot(unpack[: count * stacked], tiles.reshape(step * tile, lanes))
    return jnp.concatenate(
        [high[c * stacked : (c + 1) * stacked] for c in range(count)], axis=1
    ).astype(BF)


def kernel(
    n_group,
    n_dp,
    blk_hbm,
    prot_hbm,
    w_hbm,
    cot_hbm,
    accum_hbm,
    table_hbm,
    hid_hbm,
    got_grad,
    dense_t,
    accum,
    table,
    unpack,
    blk_ref,
    prot_ref,
    w_ref,
    cot_ref,
    hid,
    hid_t,
    send_w,
    got_w,
    send_part,
    got_part,
    send_grad,
    dense,
    part,
    pick,
    pick_t,
    sends,
    recvs,
    loads,
):
    n = n_group * n_dp
    mine = (lax.axis_index("group"), lax.axis_index("dp"))
    me = mine[0] * n_dp + mine[1]
    pairs_of = [(blk_hbm, blk_ref), (prot_hbm, prot_ref), (w_hbm, w_ref)]
    others_of = [(table_hbm, table), (hid_hbm, hid), (cot_hbm, cot_ref), (accum_hbm, accum)]
    copies = [
        pltpu.make_async_copy(a, b, loads.at[i]) for i, (a, b) in enumerate(pairs_of + others_of)
    ]
    for copy in copies[:3]:
        copy.start()
    load_pairs = copies[:3]
    load_table, load_hid, load_cot, load_accum = copies[3:]

    def to_all(act, sides=range(n_group)):
        if n <= 32:
            at_group, at_dp = flips(mine[0], n_group), flips(mine[1], n_dp)
            half = n_dp // 2
            for a in reversed(sides):
                for b in reversed(range(half)):
                    for c in (b + half, b):
                        if a or c:
                            act((at_group[a], at_dp[c]), at_group[a] * n_dp + at_dp[c])
        else:

            def one(i, carry):
                t = lax.rem(me + i, n)
                act((lax.div(t, n_dp), lax.rem(t, n_dp)), t)
                return carry

            lax.fori_loop(1, n, one, 0)

    barrier = pltpu.get_barrier_semaphore()
    to_all(
        lambda device, t: pl.semaphore_signal(
            barrier, inc=1, device_id=device, device_id_type=MESH
        )
    )

    for copy in copies[3:]:
        copy.start()

    halves = n <= 32 and n == 2 * TOGETHER
    half = lax.div(me, TOGETHER)
    far_sides, near_sides = range(n_group // 2, n_group), range(n_group // 2)

    def sending(send, got, phase, landed):
        def start(device, t):
            pltpu.make_async_remote_copy(
                src_ref=send.at[t],
                dst_ref=got.at[me],
                send_sem=sends.at[phase],
                recv_sem=recvs.at[landed],
                device_id=device,
                device_id_type=MESH,
            ).start()

        return start

    def exchange(send, got, phase, make):
        if halves:
            make(1 - half)
            to_all(sending(send, got, phase, phase), far_sides)
            make(half)
            to_all(sending(send, got, phase, phase), near_sides)
        else:
            each(make)
            to_all(sending(send, got, phase, phase))
        got[me] = send[me]

    others = pl.ds(0, n - 1)

    def arrived(got, phase):
        pltpu.make_async_copy(got.at[others], got.at[others], recvs.at[phase]).wait()

    def left(send, phase):
        pltpu.make_async_copy(send.at[others], send.at[others], sends.at[phase]).wait()

    width = table.shape[1]
    block_rows = w_ref.shape[1]
    blocks = table.shape[0] // block_rows
    chunks = width // LANES
    proteins = cot_ref.shape[0]
    pairs = w_ref.shape[0]
    tile = chunks * CAP
    slots = n * CAP
    step = min(TOGETHER, n)
    groups = n // step
    rows = step * tile
    few = groups <= 4

    def each(body):
        if few:
            for g in range(groups):
                body(g)
        else:
            lax.fori_loop(0, groups, lambda g, c: (body(g), c)[1], 0)

    def at(g, size):
        fixed = isinstance(g, int)
        return pl.ds(g * size, size) if fixed else pl.ds(pl.multiple_of(g * size, size), size)

    for copy in load_pairs:
        copy.wait()
    blk = blk_ref[...]
    owner = over(blk, blocks)
    local = rest(blk, blocks)
    local_prot = prot_ref[...] - me * proteins
    square = (pairs, pairs)
    from_row, from_col = iota(square, 0), iota(square, 1)
    owner_f = owner.astype(F32)
    owner_col = jnp.sum(jnp.where(from_row == from_col, owner_f, 0.0), axis=1, keepdims=True)
    earlier = (owner_col == owner_f) & (from_row < from_col)
    rank = jnp.sum(jnp.where(earlier, 1.0, 0.0), axis=0, keepdims=True)
    slot = owner * CAP + rank.astype(jnp.int32)

    place_rows = iota((rows, pairs), 0)
    place_slot = over(place_rows, tile) * CAP + rest(place_rows, CAP)
    weights = w_ref[...]

    def place_of(g):
        return place_slot + g * (step * CAP) == slot

    slot_rows = iota((step * CAP, pairs), 0)

    def make_w(g):
        place = slot_rows + g * (step * CAP) == slot
        block = jnp.sum(jnp.where(place, local.astype(F32), 0.0), axis=1, keepdims=True)
        marked = dot(ones_where(place), weights) * (1.0 + block * MARK)
        send_w[at(g, step)] = marked.reshape(step, CAP, block_rows)

    each(make_w)
    pl.semaphore_wait(barrier, n - 1)
    if halves:
        to_all(sending(send_w, got_w, 0, 0), far_sides)
        to_all(sending(send_w, got_w, 0, 3), near_sides)
    else:
        to_all(sending(send_w, got_w, 0, 0))
    got_w[me] = send_w[me]

    for_prot = ones_where(rest(iota((chunks * PAD, pairs), 0), PAD) == local_prot)
    shape = (chunks * PAD, rows)
    same_c = over(iota(shape, 0), PAD) == over(rest(iota(shape, 1), tile), CAP)
    shape = (rows, chunks * PAD)
    same_c_t = over(iota(shape, 1), PAD) == over(rest(iota(shape, 0), tile), CAP)

    def make_pick(g):
        place = ones_where(place_of(g))
        pick[g] = jnp.where(same_c, dot_nt(for_prot, place), 0.0).astype(BF)
        pick_t[at(g, rows), :] = jnp.where(same_c_t, dot_nt(place, for_prot), 0.0).astype(BF)

    each(make_pick)

    stacked = step * CAP
    pack, unpack[...] = repack(step, chunks)
    def make_dense(g):
        marked = got_w[at(g, step)].reshape(stacked, block_rows)
        plain = marked.astype(BF).astype(F32)
        dense[at(g, stacked), :] = jnp.concatenate(
            [jnp.where(marked == plain * (1.0 + b * MARK), plain, 0.0) for b in range(blocks)],
            axis=1,
        ).astype(BF)

    big = stacked if halves else min(slots, 256)

    def multiply(h):
        part[at(h, big), :] = dot(dense[at(h, big), :], table[...]).astype(BF)

    def make_part(g):
        own = part[at(g, stacked), :]
        stack = jnp.concatenate(
            [own[:, c * LANES : (c + 1) * LANES] for c in range(chunks)], axis=0
        )
        send_part[at(g, step)] = dot(pack, stack).astype(BF).reshape(step, tile, LANES)

    load_table.wait()
    if halves:
        for g, sides, landed, count in (
            (1 - half, far_sides, 0, step),
            (half, near_sides, 3, step - 1),
        ):
            some = got_w.at[pl.ds(0, count)]
            pltpu.make_async_copy(some, some, recvs.at[landed]).wait()
            make_dense(g)
            multiply(g)
            make_part(g)
            to_all(sending(send_part, got_part, 1, 1), sides)
        got_part[me] = send_part[me]
    else:
        arrived(got_w, 0)
        each(make_dense)
        lax.fori_loop(0, slots // big, lambda h, c: (multiply(h), c)[1], 0)
        exchange(send_part, got_part, 1, make_part)

    dense_t[...] = dense[...].astype(F32).T.astype(BF)
    load_accum.wait()
    load_hid.wait()
    for i in range(hid.shape[0] // LANES):
        some = pl.ds(i * LANES, LANES)
        hid_t[:, some] = hid[some, :].T
    arrived(got_part, 1)

    def bag_of(g):
        return dot(pick[g], got_part[at(g, step)].reshape(rows, LANES))

    if few:
        stack = sum(bag_of(g) for g in range(groups))
    else:
        stack = lax.fori_loop(
            0, groups, lambda g, c: c + bag_of(g), jnp.zeros((chunks * PAD, LANES), F32)
        )
    bag = jnp.concatenate([stack[c * PAD : (c + 1) * PAD] for c in range(chunks)], axis=1)
    load_cot.wait()
    cot = cot_ref[...].astype(F32)
    cot = jnp.concatenate([cot, jnp.zeros((PAD - proteins, cot.shape[1]), F32)], axis=0)
    inv = lax.rsqrt(jnp.mean(bag * bag, axis=-1, keepdims=True) + 1e-06)
    unit = bag * inv
    pre = dot(unit.astype(BF), hid[...])
    sig = jax.nn.sigmoid(pre)
    dpre = (cot * sig * (1.0 + pre * (1.0 - sig))).astype(BF)
    dunit = dot(dpre, hid_t[...])
    dbag = (dunit - unit * jnp.mean(dunit * unit, axis=-1, keepdims=True)) * inv
    dstack = jnp.concatenate(
        [dbag[:, c * LANES : (c + 1) * LANES] for c in range(chunks)], axis=0
    ).astype(BF)

    def make_grad(g):
        send_grad[at(g, step)] = (
            dot(pick_t[at(g, rows), :], dstack).astype(BF).reshape(step, tile, LANES)
        )

    exchange(send_grad, got_grad, 2, make_grad)
    left(send_w, 0)
    left(send_part, 1)
    left(send_grad, 2)
    arrived(got_grad, 2)


def update(
    dense_t, tiles, accum, table, unpack, out_hbm, acc_hbm, rows_out, acc_out, gathered, stores
):
    n, tile, _ = tiles.shape
    blocks, block_rows = accum.shape
    chunks = tile // CAP
    step = min(TOGETHER, n)
    groups = n // step
    stacked = step * CAP
    parts = [pl.ds(b * block_rows, block_rows) for b in range(blocks)]
    diagonal = iota((block_rows, block_rows), 0) == iota((block_rows, block_rows), 1)

    def make_gathered(g):
        few = groups <= 4
        gathered[pl.ds(g * stacked if few else pl.multiple_of(g * stacked, stacked), stacked), :] = (
            unpacked(unpack[...], tiles[pl.ds(g * step, step)], chunks)
        )

    if groups <= 4:
        for g in range(groups):
            make_gathered(g)
    else:
        lax.fori_loop(0, groups, lambda g, c: (make_gathered(g), c)[1], 0)
    writes = []
    for b, some in enumerate(parts):
        grad = dot(dense_t[some, :], gathered[...])
        mean = jnp.mean(grad * grad, axis=-1, keepdims=True)
        old = jnp.sum(jnp.where(diagonal, accum[b : b + 1, :], 0.0), axis=1, keepdims=True)
        new = old + mean
        scale = 0.3 / (jnp.sqrt(new) + 1e-08)
        rows_out[some, :] = (table[some, :].astype(F32) - grad * scale).astype(BF)
        write = pltpu.make_async_copy(rows_out.at[some], out_hbm.at[some], stores.at[b])
        write.start()
        writes.append(write)
        acc_out[b : b + 1, :] = jnp.sum(jnp.where(diagonal, new, 0.0), axis=0, keepdims=True)
    write = pltpu.make_async_copy(acc_out, acc_hbm, stores.at[blocks])
    write.start()
    writes.append(write)
    for write in writes:
        write.wait()


def per_device(table, accum, pair_block, pair_protein, pair_weight, w_hidden, hidden_cot):
    n_group = lax.axis_size("group")
    n_dp = lax.axis_size("dp")
    n = n_group * n_dp
    rows_dev, width = table.shape
    pairs, block_rows = pair_weight.shape
    blocks = rows_dev // block_rows
    tile = (width // LANES) * CAP
    slots = n * CAP
    step = min(TOGETHER, n)
    hbm = pl.BlockSpec(memory_space=pltpu.HBM)
    vmem = pl.BlockSpec(memory_space=pltpu.VMEM)
    tiles = pltpu.VMEM((n, tile, LANES), BF)
    stack = (width // LANES) * PAD
    got_grad, dense_t, accum_held, table_held, unpack = pl.pallas_call(
        functools.partial(kernel, n_group, n_dp),
        out_shape=(
            jax.ShapeDtypeStruct((n, tile, LANES), BF),
            jax.ShapeDtypeStruct((rows_dev, slots), BF),
            jax.ShapeDtypeStruct((blocks, block_rows), F32),
            jax.ShapeDtypeStruct(table.shape, BF),
            jax.ShapeDtypeStruct((step * tile, step * tile), BF),
        ),
        in_specs=[hbm] * 7,
        out_specs=(vmem,) * 5,
        scratch_shapes=[
            pltpu.VMEM((1, pairs), jnp.int32),
            pltpu.VMEM((1, pairs), jnp.int32),
            pltpu.VMEM(pair_weight.shape, BF),
            pltpu.VMEM(hidden_cot.shape, BF),
            pltpu.VMEM(w_hidden.shape, BF),
            pltpu.VMEM(w_hidden.shape[::-1], BF),
            pltpu.VMEM((n, CAP, block_rows), F32),
            pltpu.VMEM((n, CAP, block_rows), F32),
            tiles,
            tiles,
            tiles,
            pltpu.VMEM((slots, rows_dev), BF),
            pltpu.VMEM((slots, width), BF),
            pltpu.VMEM((n // step, stack, step * tile), BF),
            pltpu.VMEM((n * tile, stack), BF),
            pltpu.SemaphoreType.DMA((3,)),
            pltpu.SemaphoreType.DMA((4,)),
            pltpu.SemaphoreType.DMA((7,)),
        ],
        compiler_params=pltpu.CompilerParams(
            collective_id=0, has_side_effects=True, vmem_limit_bytes=LIMIT
        ),
        name="bags",
    )(
        *(
            pltpu.with_memory_space_constraint(x, pltpu.HBM)
            for x in (
                pair_block.reshape(1, pairs),
                pair_protein.reshape(1, pairs),
                pair_weight,
                hidden_cot,
                accum.reshape(blocks, block_rows),
                table,
                w_hidden,
            )
        )
    )
    new_table, new_accum = pl.pallas_call(
        update,
        out_shape=(
            jax.ShapeDtypeStruct(table.shape, BF),
            jax.ShapeDtypeStruct((blocks, block_rows), F32),
        ),
        in_specs=[vmem] * 5,
        out_specs=(hbm, hbm),
        scratch_shapes=[
            pltpu.VMEM(table.shape, BF),
            pltpu.VMEM((blocks, block_rows), F32),
            pltpu.VMEM((slots, width), BF),
            pltpu.SemaphoreType.DMA((1 + blocks,)),
        ],
        compiler_params=pltpu.CompilerParams(vmem_limit_bytes=LIMIT // 2),
        name="update",
    )(dense_t, got_grad, accum_held, table_held, unpack)
    return new_table, new_accum.reshape(rows_dev)


def solution(mesh):
    in_specs = (
        P(("group", "dp"), None),
        P(("group", "dp")),
        P(("group", "dp")),
        P(("group", "dp")),
        P(("group", "dp"), None),
        P(),
        P(("group", "dp"), None),
    )
    out_specs = (P(("group", "dp"), None), P(("group", "dp")))
    return jax.shard_map(
        per_device, mesh=mesh, in_specs=in_specs, out_specs=out_specs, check_vma=False
    )
```

```python
import functools

import jax
import jax.numpy as jnp
from jax import lax
from jax.experimental import pallas as pl
from jax.experimental.pallas import tpu as pltpu
from jax.sharding import PartitionSpec as P

CAP = 2
LANES = 128
TOGETHER = 16
PAD = 8
MARK = 2.0**-15
LIMIT = 40 * 1024 * 1024
MESH = pl.DeviceIdType.MESH
BF = jnp.bfloat16
F32 = jnp.float32


def dot(a, b):
    return jnp.dot(a, b, preferred_element_type=F32)


def dot_nt(a, b):
    return lax.dot_general(a, b, (((1,), (1,)), ((), ())), preferred_element_type=F32)


def iota(shape, dim):
    return lax.broadcasted_iota(jnp.int32, shape, dim)


def over(x, k):
    return jnp.right_shift(x, k.bit_length() - 1)


def rest(x, k):
    return jnp.bitwise_and(x, k - 1)


def flips(x, count):
    found = [x]
    k = 1
    while k < count:
        change = k * (1 - 2 * lax.rem(lax.div(x, k), 2))
        found += [y + change for y in found]
        k *= 2
    return found


def ones_where(mask):
    return jnp.where(mask, 1.0, 0.0).astype(BF)


def repack(step, chunks):
    tile, stacked = chunks * CAP, step * CAP
    shape = (step * tile, step * tile)
    to_r, to_c = iota(shape, 0), iota(shape, 1)
    r_c, r_d, r_k = over(to_r, stacked), over(rest(to_r, stacked), CAP), rest(to_r, CAP)
    unpack = ones_where(to_c == r_d * tile + r_c * CAP + r_k)
    t_c, t_d, t_k = over(to_c, stacked), over(rest(to_c, stacked), CAP), rest(to_c, CAP)
    pack = ones_where(to_r == t_d * tile + t_c * CAP + t_k)
    return pack, unpack


def unpacked(unpack, tiles, count):
    step, tile, lanes = tiles.shape
    stacked = step * CAP
    high = dot(unpack[: count * stacked], tiles.reshape(step * tile, lanes))
    return jnp.concatenate(
        [high[c * stacked : (c + 1) * stacked] for c in range(count)], axis=1
    ).astype(BF)


def kernel(
    n_group,
    n_dp,
    blk_hbm,
    prot_hbm,
    w_hbm,
    cot_hbm,
    accum_hbm,
    table_hbm,
    hid_hbm,
    got_grad,
    dense_t,
    accum,
    table,
    unpack,
    blk_ref,
    prot_ref,
    w_ref,
    cot_ref,
    hid,
    hid_t,
    send_w,
    got_w,
    send_part,
    got_part,
    send_grad,
    dense,
    part,
    pick,
    pick_t,
    sends,
    recvs,
    loads,
):
    n = n_group * n_dp
    mine = (lax.axis_index("group"), lax.axis_index("dp"))
    me = mine[0] * n_dp + mine[1]
    pairs_of = [(blk_hbm, blk_ref), (prot_hbm, prot_ref), (w_hbm, w_ref)]
    others_of = [(table_hbm, table), (hid_hbm, hid), (cot_hbm, cot_ref), (accum_hbm, accum)]
    copies = [
        pltpu.make_async_copy(a, b, loads.at[i]) for i, (a, b) in enumerate(pairs_of + others_of)
    ]
    for copy in copies[:3]:
        copy.start()
    load_pairs = copies[:3]
    load_table, load_hid, load_cot, load_accum = copies[3:]

    def to_all(act, sides=range(n_group)):
        if n <= 32:
            at_group, at_dp = flips(mine[0], n_group), flips(mine[1], n_dp)
            middle = n_dp // 2
            for b in reversed(range(middle)):
                for a in reversed(sides):
                    for c in (b + middle, b):
                        if a or c:
                            act((at_group[a], at_dp[c]), at_group[a] * n_dp + at_dp[c])
        else:

            def one(i, carry):
                t = lax.rem(me + i, n)
                act((lax.div(t, n_dp), lax.rem(t, n_dp)), t)
                return carry

            lax.fori_loop(1, n, one, 0)

    barrier = pltpu.get_barrier_semaphore()
    to_all(
        lambda device, t: pl.semaphore_signal(
            barrier, inc=1, device_id=device, device_id_type=MESH
        )
    )

    for copy in copies[3:]:
        copy.start()

    halves = n <= 32 and n == 2 * TOGETHER
    half = lax.div(me, TOGETHER)
    far_sides, near_sides = range(n_group // 2, n_group), range(n_group // 2)

    def sending(send, got, phase, landed):
        def start(device, t):
            pltpu.make_async_remote_copy(
                src_ref=send.at[t],
                dst_ref=got.at[me],
                send_sem=sends.at[phase],
                recv_sem=recvs.at[landed],
                device_id=device,
                device_id_type=MESH,
            ).start()

        return start

    def exchange(send, got, phase, make):
        if halves:
            make(1 - half)
            to_all(sending(send, got, phase, phase), far_sides)
            make(half)
            to_all(sending(send, got, phase, phase), near_sides)
        else:
            each(make)
            to_all(sending(send, got, phase, phase))
        got[me] = send[me]

    others = pl.ds(0, n - 1)

    def arrived(got, phase):
        pltpu.make_async_copy(got.at[others], got.at[others], recvs.at[phase]).wait()

    def left(send, phase):
        pltpu.make_async_copy(send.at[others], send.at[others], sends.at[phase]).wait()

    width = table.shape[1]
    block_rows = w_ref.shape[1]
    blocks = table.shape[0] // block_rows
    chunks = width // LANES
    proteins = cot_ref.shape[0]
    pairs = w_ref.shape[0]
    tile = chunks * CAP
    slots = n * CAP
    step = min(TOGETHER, n)
    groups = n // step
    rows = step * tile
    few = groups <= 4

    def each(body):
        if few:
            for g in range(groups):
                body(g)
        else:
            lax.fori_loop(0, groups, lambda g, c: (body(g), c)[1], 0)

    def at(g, size):
        fixed = isinstance(g, int)
        return pl.ds(g * size, size) if fixed else pl.ds(pl.multiple_of(g * size, size), size)

    for copy in load_pairs:
        copy.wait()
    blk = blk_ref[...]
    owner = over(blk, blocks)
    local = rest(blk, blocks)
    local_prot = prot_ref[...] - me * proteins
    square = (pairs, pairs)
    from_row, from_col = iota(square, 0), iota(square, 1)
    owner_f = owner.astype(F32)
    owner_col = jnp.sum(jnp.where(from_row == from_col, owner_f, 0.0), axis=1, keepdims=True)
    earlier = (owner_col == owner_f) & (from_row < from_col)
    rank = jnp.sum(jnp.where(earlier, 1.0, 0.0), axis=0, keepdims=True)
    slot = owner * CAP + rank.astype(jnp.int32)

    place_rows = iota((rows, pairs), 0)
    place_slot = over(place_rows, tile) * CAP + rest(place_rows, CAP)
    weights = w_ref[...]

    def place_of(g):
        return place_slot + g * (step * CAP) == slot

    slot_rows = iota((step * CAP, pairs), 0)

    def make_w(g):
        place = slot_rows + g * (step * CAP) == slot
        block = jnp.sum(jnp.where(place, local.astype(F32), 0.0), axis=1, keepdims=True)
        marked = dot(ones_where(place), weights) * (1.0 + block * MARK)
        send_w[at(g, step)] = marked.reshape(step, CAP, block_rows)

    each(make_w)
    pl.semaphore_wait(barrier, n - 1)
    if halves:
        to_all(sending(send_w, got_w, 0, 0), far_sides)
        to_all(sending(send_w, got_w, 0, 3), near_sides)
    else:
        to_all(sending(send_w, got_w, 0, 0))
    got_w[me] = send_w[me]

    for_prot = ones_where(rest(iota((chunks * PAD, pairs), 0), PAD) == local_prot)
    shape = (chunks * PAD, rows)
    same_c = over(iota(shape, 0), PAD) == over(rest(iota(shape, 1), tile), CAP)
    shape = (rows, chunks * PAD)
    same_c_t = over(iota(shape, 1), PAD) == over(rest(iota(shape, 0), tile), CAP)

    def make_pick(g):
        place = ones_where(place_of(g))
        pick[g] = jnp.where(same_c, dot_nt(for_prot, place), 0.0).astype(BF)
        pick_t[at(g, rows), :] = jnp.where(same_c_t, dot_nt(place, for_prot), 0.0).astype(BF)

    each(make_pick)

    stacked = step * CAP
    pack, unpack[...] = repack(step, chunks)
    def make_dense(g):
        marked = got_w[at(g, step)].reshape(stacked, block_rows)
        plain = marked.astype(BF).astype(F32)
        dense[at(g, stacked), :] = jnp.concatenate(
            [jnp.where(marked == plain * (1.0 + b * MARK), plain, 0.0) for b in range(blocks)],
            axis=1,
        ).astype(BF)

    big = stacked if halves else min(slots, 256)

    def multiply(h):
        part[at(h, big), :] = dot(dense[at(h, big), :], table[...]).astype(BF)

    def make_part(g):
        own = part[at(g, stacked), :]
        stack = jnp.concatenate(
            [own[:, c * LANES : (c + 1) * LANES] for c in range(chunks)], axis=0
        )
        send_part[at(g, step)] = dot(pack, stack).astype(BF).reshape(step, tile, LANES)

    load_table.wait()
    if halves:
        for g, sides, landed, count in (
            (1 - half, far_sides, 0, step),
            (half, near_sides, 3, step - 1),
        ):
            some = got_w.at[pl.ds(0, count)]
            pltpu.make_async_copy(some, some, recvs.at[landed]).wait()
            make_dense(g)
            multiply(g)
            make_part(g)
            to_all(sending(send_part, got_part, 1, 1), sides)
        got_part[me] = send_part[me]
    else:
        arrived(got_w, 0)
        each(make_dense)
        lax.fori_loop(0, slots // big, lambda h, c: (multiply(h), c)[1], 0)
        exchange(send_part, got_part, 1, make_part)

    dense_t[...] = dense[...].astype(F32).T.astype(BF)
    load_accum.wait()
    load_hid.wait()
    for i in range(hid.shape[0] // LANES):
        some = pl.ds(i * LANES, LANES)
        hid_t[:, some] = hid[some, :].T
    arrived(got_part, 1)

    def bag_of(g):
        return dot(pick[g], got_part[at(g, step)].reshape(rows, LANES))

    if few:
        stack = sum(bag_of(g) for g in range(groups))
    else:
        stack = lax.fori_loop(
            0, groups, lambda g, c: c + bag_of(g), jnp.zeros((chunks * PAD, LANES), F32)
        )
    bag = jnp.concatenate([stack[c * PAD : (c + 1) * PAD] for c in range(chunks)], axis=1)
    load_cot.wait()
    cot = cot_ref[...].astype(F32)
    cot = jnp.concatenate([cot, jnp.zeros((PAD - proteins, cot.shape[1]), F32)], axis=0)
    inv = lax.rsqrt(jnp.mean(bag * bag, axis=-1, keepdims=True) + 1e-06)
    unit = bag * inv
    pre = dot(unit.astype(BF), hid[...])
    sig = jax.nn.sigmoid(pre)
    dpre = (cot * sig * (1.0 + pre * (1.0 - sig))).astype(BF)
    dunit = dot(dpre, hid_t[...])
    dbag = (dunit - unit * jnp.mean(dunit * unit, axis=-1, keepdims=True)) * inv
    dstack = jnp.concatenate(
        [dbag[:, c * LANES : (c + 1) * LANES] for c in range(chunks)], axis=0
    ).astype(BF)

    def make_grad(g):
        send_grad[at(g, step)] = (
            dot(pick_t[at(g, rows), :], dstack).astype(BF).reshape(step, tile, LANES)
        )

    exchange(send_grad, got_grad, 2, make_grad)
    left(send_w, 0)
    left(send_part, 1)
    left(send_grad, 2)
    arrived(got_grad, 2)


def update(
    dense_t, tiles, accum, table, unpack, out_hbm, acc_hbm, rows_out, acc_out, gathered, stores
):
    n, tile, _ = tiles.shape
    blocks, block_rows = accum.shape
    chunks = tile // CAP
    step = min(TOGETHER, n)
    groups = n // step
    stacked = step * CAP
    parts = [pl.ds(b * block_rows, block_rows) for b in range(blocks)]
    diagonal = iota((block_rows, block_rows), 0) == iota((block_rows, block_rows), 1)

    def make_gathered(g):
        few = groups <= 4
        gathered[pl.ds(g * stacked if few else pl.multiple_of(g * stacked, stacked), stacked), :] = (
            unpacked(unpack[...], tiles[pl.ds(g * step, step)], chunks)
        )

    if groups <= 4:
        for g in range(groups):
            make_gathered(g)
    else:
        lax.fori_loop(0, groups, lambda g, c: (make_gathered(g), c)[1], 0)
    writes = []
    for b, some in enumerate(parts):
        grad = dot(dense_t[some, :], gathered[...])
        mean = jnp.mean(grad * grad, axis=-1, keepdims=True)
        old = jnp.sum(jnp.where(diagonal, accum[b : b + 1, :], 0.0), axis=1, keepdims=True)
        new = old + mean
        scale = 0.3 / (jnp.sqrt(new) + 1e-08)
        rows_out[some, :] = (table[some, :].astype(F32) - grad * scale).astype(BF)
        write = pltpu.make_async_copy(rows_out.at[some], out_hbm.at[some], stores.at[b])
        write.start()
        writes.append(write)
        acc_out[b : b + 1, :] = jnp.sum(jnp.where(diagonal, new, 0.0), axis=0, keepdims=True)
    write = pltpu.make_async_copy(acc_out, acc_hbm, stores.at[blocks])
    write.start()
    writes.append(write)
    for write in writes:
        write.wait()


def per_device(table, accum, pair_block, pair_protein, pair_weight, w_hidden, hidden_cot):
    n_group = lax.axis_size("group")
    n_dp = lax.axis_size("dp")
    n = n_group * n_dp
    rows_dev, width = table.shape
    pairs, block_rows = pair_weight.shape
    blocks = rows_dev // block_rows
    tile = (width // LANES) * CAP
    slots = n * CAP
    step = min(TOGETHER, n)
    hbm = pl.BlockSpec(memory_space=pltpu.HBM)
    vmem = pl.BlockSpec(memory_space=pltpu.VMEM)
    tiles = pltpu.VMEM((n, tile, LANES), BF)
    stack = (width // LANES) * PAD
    got_grad, dense_t, accum_held, table_held, unpack = pl.pallas_call(
        functools.partial(kernel, n_group, n_dp),
        out_shape=(
            jax.ShapeDtypeStruct((n, tile, LANES), BF),
            jax.ShapeDtypeStruct((rows_dev, slots), BF),
            jax.ShapeDtypeStruct((blocks, block_rows), F32),
            jax.ShapeDtypeStruct(table.shape, BF),
            jax.ShapeDtypeStruct((step * tile, step * tile), BF),
        ),
        in_specs=[hbm] * 7,
        out_specs=(vmem,) * 5,
        scratch_shapes=[
            pltpu.VMEM((1, pairs), jnp.int32),
            pltpu.VMEM((1, pairs), jnp.int32),
            pltpu.VMEM(pair_weight.shape, BF),
            pltpu.VMEM(hidden_cot.shape, BF),
            pltpu.VMEM(w_hidden.shape, BF),
            pltpu.VMEM(w_hidden.shape[::-1], BF),
            pltpu.VMEM((n, CAP, block_rows), F32),
            pltpu.VMEM((n, CAP, block_rows), F32),
            tiles,
            tiles,
            tiles,
            pltpu.VMEM((slots, rows_dev), BF),
            pltpu.VMEM((slots, width), BF),
            pltpu.VMEM((n // step, stack, step * tile), BF),
            pltpu.VMEM((n * tile, stack), BF),
            pltpu.SemaphoreType.DMA((3,)),
            pltpu.SemaphoreType.DMA((4,)),
            pltpu.SemaphoreType.DMA((7,)),
        ],
        compiler_params=pltpu.CompilerParams(
            collective_id=0, has_side_effects=True, vmem_limit_bytes=LIMIT
        ),
        name="bags",
    )(
        *(
            pltpu.with_memory_space_constraint(x, pltpu.HBM)
            for x in (
                pair_block.reshape(1, pairs),
                pair_protein.reshape(1, pairs),
                pair_weight,
                hidden_cot,
                accum.reshape(blocks, block_rows),
                table,
                w_hidden,
            )
        )
    )
    new_table, new_accum = pl.pallas_call(
        update,
        out_shape=(
            jax.ShapeDtypeStruct(table.shape, BF),
            jax.ShapeDtypeStruct((blocks, block_rows), F32),
        ),
        in_specs=[vmem] * 5,
        out_specs=(hbm, hbm),
        scratch_shapes=[
            pltpu.VMEM(table.shape, BF),
            pltpu.VMEM((blocks, block_rows), F32),
            pltpu.VMEM((slots, width), BF),
            pltpu.SemaphoreType.DMA((1 + blocks,)),
        ],
        compiler_params=pltpu.CompilerParams(vmem_limit_bytes=LIMIT // 2),
        name="update",
    )(dense_t, got_grad, accum_held, table_held, unpack)
    return new_table, new_accum.reshape(rows_dev)


def solution(mesh):
    in_specs = (
        P(("group", "dp"), None),
        P(("group", "dp")),
        P(("group", "dp")),
        P(("group", "dp")),
        P(("group", "dp"), None),
        P(),
        P(("group", "dp"), None),
    )
    out_specs = (P(("group", "dp"), None), P(("group", "dp")))
    return jax.shard_map(
        per_device, mesh=mesh, in_specs=in_specs, out_specs=out_specs, check_vma=False
    )
```
